128 devices in a mesh: ty: 16 (over x, y), tx: 8 (over z, core).
Axes of the slice: x: 4, y: 4, z: 4, core: 2. Of those that a mesh axis runs over, the one named last changes fastest.
Arguments:
- object_field: float32 [2, 12288, 4096], P(None, 'ty', 'tx'), may hold values from -6 to 6
- probe: float32 [2, 256, 256], replicated, may hold values from -6 to 6
- slot_counts: int32 [16, 8], P('ty', 'tx'), may hold values from 1 to 24, as said below
- positions: int32 [16, 8, 2, 24], P('ty', 'tx'), may hold values from 0 to 12032, as said below
- amplitude: float32 [16, 8, 24, 256, 256], P('ty', 'tx'), may hold values from 0.2 to 3
Outputs:
- new_object: float32 [2, 12288, 4096], P(None, 'ty', 'tx')
- new_probe: float32 [2, 256, 256], replicated
The draws below stay inside these ranges and needn't reach their ends.
Inputs may be any that keep to these rules, and one draw needn't show every extreme that they name: Each tile has at least one live slot and some tile has exactly 24; slots at index slot_counts or above are unused. `positions`: A slot's corner lies inside the tile that holds the slot, and its 256 x 256 patch lies inside the object; the patch may reach into the tiles below and to the right.
All inputs are finite; a program needn't handle non-finite values.
Results may differ from the reference program's by a relative error of at most 0.0001.
Values sent between devices are 32-bit elements; how exact they have to be, the bound alone decides.
No kernel may reach another device: no remote copies, remote signals or barrier semaphores. Data moves between devices by JAX's collectives and lax.ppermute only.
A program may use at most 128 MiB of HBM per device.

```python
import jax
import jax.numpy as jnp
from jax import lax

P_SIZE = 256
TR = 768
TC = 512
CAP = 24
NR = 12288
NC = 4096
N_TY = 16
N_TX = 8


def draw_slot_counts(key, part):
    key = jax.random.fold_in(key, 11)
    raw = jax.random.randint(key, (N_TY, N_TX), 0, CAP)
    counts = 1 + raw * raw // CAP
    pick = jax.random.randint(jax.random.fold_in(key, 5), (), 0, N_TY * N_TX)
    counts = counts.reshape(-1).at[pick].set(CAP).reshape(N_TY, N_TX)
    return counts.astype(jnp.int32)


def draw_positions(key, part):
    key = jax.random.fold_in(key, 23)
    row_key = jax.random.fold_in(key, 1)
    col_key = jax.random.fold_in(key, 2)
    tile_rows = jnp.arange(N_TY, dtype=jnp.int32)
    tile_cols = jnp.arange(N_TX, dtype=jnp.int32)
    row_limit = jnp.where(tile_rows == N_TY - 1, TR - P_SIZE + 1, TR)[:, None, None]
    col_limit = jnp.where(tile_cols == N_TX - 1, TC - P_SIZE + 1, TC)[None, :, None]
    shape = (N_TY, N_TX, CAP)
    row_off = jax.random.randint(row_key, shape, 0, jnp.broadcast_to(row_limit, shape))
    col_off = jax.random.randint(col_key, shape, 0, jnp.broadcast_to(col_limit, shape))
    row_off = row_off.at[0, 0, 0].set(0).at[N_TY - 1, N_TX - 1, 0].set(TR - P_SIZE)
    col_off = col_off.at[0, 0, 0].set(0).at[N_TY - 1, N_TX - 1, 0].set(TC - P_SIZE)
    rows = row_off + tile_rows[:, None, None] * TR
    cols = col_off + tile_cols[None, :, None] * TC
    return jnp.stack([rows, cols], axis=2).astype(jnp.int32)


def levels(stream_key, dims, pieces, smallest, high):
    def one(axis_at, blocks):
        steps = jax.random.uniform(jax.random.fold_in(jax.random.fold_in(stream_key, 6), axis_at), (blocks,), jnp.float32, smallest / len(pieces), high / len(pieces))
        return jnp.repeat(jnp.exp(steps), dims[axis_at] // blocks).reshape((-1,) + (1,) * (len(dims) - axis_at - 1))

    level = one(*pieces[0])
    for cut in pieces[1:]:
        level = level * one(*cut)
    return level


def centred(rng, extent, width, bound, split=(), held_as=jnp.bfloat16):
    entries = width * jax.random.normal(rng, extent, jnp.float32)
    if split:
        entries = entries * levels(rng, extent, split, -0.22, 0.18)
    return jnp.clip(entries, -bound, bound).astype(held_as)


def setup_inputs(seed: int = 0) -> dict:
    streams_of = jax.random.split(jax.random.key(seed), 6)
    object_field = centred(streams_of[0], (2, NR, NC), 1.0, 6.0, ((1, 16), (2, 8)), jnp.float32)
    probe = centred(streams_of[1], (2, P_SIZE, P_SIZE), 1.0, 6.0, (), jnp.float32)
    slot_counts = draw_slot_counts(jax.random.fold_in(streams_of[5], 71), 0)
    positions = draw_positions(jax.random.fold_in(streams_of[5], 71), 0)
    amplitude = jnp.clip(0.2 + 2.8 * jax.random.uniform(streams_of[4], (N_TY, N_TX, CAP, P_SIZE, P_SIZE), jnp.float32) ** levels(streams_of[4], (N_TY, N_TX, CAP, P_SIZE, P_SIZE), ((0, 16), (1, 8)), -0.2, 0.2), 0.2, 3.0)
    return dict(object_field=object_field, probe=probe, slot_counts=slot_counts, positions=positions, amplitude=amplitude)


def reference(object_field, probe, slot_counts, positions, amplitude):
    pr = probe[0]
    pi = probe[1]
    corners = jnp.transpose(positions, (0, 1, 3, 2)).reshape(-1, 2).astype(jnp.int32)
    slot_index = jnp.arange(CAP, dtype=jnp.int32)
    live = (slot_index[None, None, :] < slot_counts[:, :, None]).reshape(-1)
    amps = amplitude.reshape(-1, P_SIZE, P_SIZE)
    illum_patch = pr * pr + pi * pi

    def step(carry, item):
        acc, pnum, pden = carry
        corner, alive, amp = item
        weight = alive.astype(object_field.dtype)
        r = corner[0]
        c = corner[1]
        zero = jnp.zeros((), jnp.int32)
        patch = lax.dynamic_slice(object_field, (zero, r, c), (2, P_SIZE, P_SIZE))
        orr = patch[0]
        oi = patch[1]
        er = pr * orr - pi * oi
        ei = pr * oi + pi * orr
        far = jnp.fft.fft2(lax.complex(er, ei), norm='ortho')
        fr = jnp.real(far)
        fi = jnp.imag(far)
        scale = amp / jnp.sqrt(fr * fr + fi * fi + 0.25) - 1.0
        back = jnp.fft.ifft2(lax.complex(fr * scale, fi * scale), norm='ortho')
        wr = jnp.real(back)
        wi = jnp.imag(back)
        grad = jnp.stack([pr * wr + pi * wi, pr * wi - pi * wr, illum_patch]) * weight
        current = lax.dynamic_slice(acc, (zero, r, c), (3, P_SIZE, P_SIZE))
        acc = lax.dynamic_update_slice(acc, current + grad, (zero, r, c))
        pnum = pnum + weight * jnp.stack([orr * wr + oi * wi, orr * wi - oi * wr])
        pden = pden + weight * (orr * orr + oi * oi)
        return ((acc, pnum, pden), None)
    acc0 = jnp.zeros((3, NR, NC), object_field.dtype)
    pnum0 = jnp.zeros((2, P_SIZE, P_SIZE), object_field.dtype)
    pden0 = jnp.zeros((P_SIZE, P_SIZE), object_field.dtype)
    (acc, pnum, pden), unused = lax.scan(step, (acc0, pnum0, pden0), (corners, live, amps))
    new_object = object_field + acc[0:2] / (acc[2][None] + 1.0)
    new_probe = probe + pnum / (pden[None] + 1.0)
    return (new_object, new_probe)
```

```python
import functools

import jax
import jax.numpy as jnp
import ml_dtypes
import numpy as np
from jax import lax
from jax.experimental import pallas as pl
from jax.experimental.pallas import tpu as pltpu
from jax.sharding import PartitionSpec as P

SIZE = 256
HALF = 128
ROWS = 768
COLS = 512
CAP = 24
CH = 16
AXES = ("ty", "tx")
VMEM_LIMIT = 56 * 1024 * 1024


def halves(matrix):
    high = matrix.astype(ml_dtypes.bfloat16)
    low = (matrix - high.astype(np.float64)).astype(ml_dtypes.bfloat16)
    return high, low


def left_table(m):
    real = np.block([[m.real, -m.imag], [m.imag, m.real]])
    high, low = halves(real)
    return np.concatenate([high, high, low], 1)


def right_table(m):
    real = np.block([[m.real, m.imag], [-m.imag, m.real]])
    high, low = halves(real)
    return np.concatenate([high, high, low], 0)


@functools.lru_cache(maxsize=None)
def tables():
    n = np.arange(HALF)
    even = 2 * n
    odd_row = 2 * n + 1
    odd_col = 2 * ((n + HALF // 2) % HALF) + 1

    def dft(freq):
        turns = (freq[:, None] * n[None, :]) % SIZE
        return np.exp(-2j * np.pi * turns / SIZE) / np.sqrt(SIZE)

    left = np.stack(
        [
            left_table(dft(even)),
            left_table(dft(odd_row)),
            left_table(np.conj(dft(even)).T),
            left_table(np.conj(dft(odd_row)).T),
        ]
    )
    right = np.stack(
        [
            right_table(dft(even).T),
            right_table(dft(odd_col).T),
            right_table(np.conj(dft(even))),
            right_table(np.conj(dft(odd_col))),
        ]
    )
    return left, right


def split(x):
    high = x.astype(jnp.bfloat16)
    low = (x - high.astype(jnp.float32)).astype(jnp.bfloat16)
    return high, low


def dot(a, b):
    return jnp.dot(a, b, preferred_element_type=jnp.float32)


def lanes(rows):
    return lax.broadcasted_iota(jnp.int32, (rows, HALF), 1)


def corner_of(pos_ref, k):
    row = lax.rem(pos_ref[0, k], ROWS)
    col = lax.rem(pos_ref[1, k], COLS)
    return row, lax.div(col, HALF), lax.rem(col, HALF)


def rolled(a, b, s, low_first):
    ra = pltpu.roll(a, s, 1)
    rb = pltpu.roll(b, s, 1)
    return jnp.where(low_first, ra, rb), jnp.where(low_first, rb, ra)


def illum_kernel(count_ref, pos_ref, probe_ref, acc_ref, power):
    acc_ref[...] = jnp.zeros_like(acc_ref)
    for j in range(2):
        re = probe_ref[0, :, HALF * j : HALF * (j + 1)]
        im = probe_ref[1, :, HALF * j : HALF * (j + 1)]
        power[j] = re * re + im * im

    def body(k, carry):
        row, tile, s = corner_of(pos_ref, k)
        for i in range(0, SIZE, CH):
            ge = lanes(CH) >= s
            p0, p1 = rolled(power[0, i : i + CH], power[1, i : i + CH], s, ge)
            at = pl.ds(row + i, CH)
            acc_ref[tile, at, :] += jnp.where(ge, p0, 0.0)
            acc_ref[tile + 1, at, :] += p1
            acc_ref[tile + 2, at, :] += jnp.where(ge, 0.0, p0)
        return carry

    lax.fori_loop(0, count_ref[0, 0], body, 0)


def slots_kernel(
    count_ref, pos_ref, own_ref, east_ref, south_ref, corner_ref, amp_ref, probe_ref, left_ref, right_ref,
    acc_ref, sums_ref,
    ext, prob, patch, xs, ys, zs, fs, amp, piece_sem, amp_sem,
):
    count = count_ref[0, 0]

    def amp_copies(k, slot):
        return [
            pltpu.make_async_copy(amp_ref.at[k, :, pl.ds(HALF * j, HALF)], amp.at[slot, j], amp_sem.at[slot, j])
            for j in range(2)
        ]

    for copy in amp_copies(0, 0):
        copy.start()
    pieces = []
    for c in range(2):
        for t in range(6):
            for below in range(2):
                if t < 4:
                    source = (south_ref if below else own_ref).at[c, :, pl.ds(HALF * t, HALF)]
                else:
                    source = (corner_ref if below else east_ref).at[c, :, pl.ds(HALF * (t - 4), HALF)]
                target = ext.at[c, t, pl.ds(ROWS, SIZE) if below else pl.ds(0, ROWS)]
                pieces.append(pltpu.make_async_copy(source, target, piece_sem.at[len(pieces)]))
    for copy in pieces:
        copy.start()
    acc_ref[...] = jnp.zeros_like(acc_ref)
    sums_ref[...] = jnp.zeros_like(sums_ref)
    for copy in pieces:
        copy.wait()

    def body(k, carry):
        slot = lax.rem(k, 2)

        @pl.when(k + 1 < count)
        def _():
            for copy in amp_copies(k + 1, 1 - slot):
                copy.start()

        row, tile, s = corner_of(pos_ref, k)
        ge = lanes(CH) >= s
        for i in range(0, HALF, CH):
            waves = []
            for h in range(2):
                at = HALF * h + i
                span = slice(at, at + CH)
                pr = rolled(probe_ref[0, span, :HALF], probe_ref[0, span, HALF:], s, ge)
                pi = rolled(probe_ref[1, span, :HALF], probe_ref[1, span, HALF:], s, ge)
                where = pl.ds(row + at, CH)
                obj = []
                for c in range(2):
                    first = jnp.where(ge, ext[c, tile, where, :], ext[c, tile + 2, where, :])
                    obj.append((first, ext[c, tile + 1, where, :]))
                for j in range(2):
                    prob[0, j, span] = pr[j]
                    prob[1, j, span] = pi[j]
                    patch[0, j, span] = obj[0][j]
                    patch[1, j, span] = obj[1][j]
                waves.append(
                    [
                        (pr[j] * obj[0][j] - pi[j] * obj[1][j], pr[j] * obj[1][j] + pi[j] * obj[0][j])
                        for j in range(2)
                    ]
                )
            for j in range(2):
                col = slice(HALF * j, HALF * (j + 1))
                for c in range(2):
                    top, low = waves[0][j][c], waves[1][j][c]
                    for p, value in ((0, top + low), (1, top - low)):
                        hi, lo = split(value)
                        xs[p, HALF * c + i : HALF * c + i + CH, col] = hi
                        xs[p, SIZE + HALF * c + i : SIZE + HALF * c + i + CH, col] = lo

        def left_dot(table, p):
            ys[p] = dot(left_ref[table, :, : 2 * SIZE], xs[p]) + dot(left_ref[table, :, 2 * SIZE :], xs[p, :SIZE])

        def right_dot(table, p):
            fs[p] = dot(zs[p], right_ref[table, : 2 * SIZE]) + dot(zs[p, :, :SIZE], right_ref[table, 2 * SIZE :])

        def put_z(p, rows, c, value):
            hi, lo = split(value)
            zs[p, rows, HALF * c : HALF * (c + 1)] = hi
            zs[p, rows, SIZE + HALF * c : SIZE + HALF * (c + 1)] = lo

        left_dot(0, 0)
        left_dot(1, 1)
        for r in range(2):
            for i in range(0, HALF, CH):
                rows = slice(HALF * r + i, HALF * r + i + CH)
                for c in range(2):
                    span = slice(HALF * c + i, HALF * c + i + CH)
                    a, b = ys[r, span, :HALF], ys[r, span, HALF:]
                    put_z(0, rows, c, a + b)
                    put_z(1, rows, c, a - b)
        right_dot(0, 0)
        right_dot(1, 1)
        for copy in amp_copies(k, slot):
            copy.wait()
        lane = lanes(CH)
        near = lane < HALF // 2
        pick0 = jnp.where(near, 2 * lane, 2 * lane - (HALF - 1))
        pick1 = jnp.where(near, 2 * lane + 1, 2 * lane - HALF)
        for r in range(2):
            for i in range(0, HALF, CH):
                rows = slice(HALF * r + i, HALF * r + i + CH)
                a0 = amp[slot, 0, pl.ds(2 * i + r, CH, stride=2), :]
                a1 = amp[slot, 1, pl.ds(2 * i + r, CH, stride=2), :]
                v0 = jnp.take_along_axis(a0, pick0, axis=1)
                v1 = jnp.take_along_axis(a1, pick1, axis=1)
                for p, value in ((0, jnp.where(near, v0, v1)), (1, jnp.where(near, v1, v0))):
                    fr, fi = fs[p, rows, :HALF], fs[p, rows, HALF:]
                    scale = value * lax.rsqrt(fr * fr + fi * fi + 0.25) - 1.0
                    put_z(p, rows, 0, fr * scale)
                    put_z(p, rows, 1, fi * scale)
        right_dot(2, 0)
        right_dot(3, 1)
        for r in range(2):
            for i in range(0, HALF, CH):
                rows = slice(HALF * r + i, HALF * r + i + CH)
                for c in range(2):
                    lane_part = slice(HALF * c, HALF * (c + 1))
                    a, b = fs[0, rows, lane_part], fs[1, rows, lane_part]
                    for j, value in ((0, a + b), (1, a - b)):
                        hi, lo = split(value)
                        col = slice(HALF * j, HALF * (j + 1))
                        xs[r, HALF * c + i : HALF * c + i + CH, col] = hi
                        xs[r, SIZE + HALF * c + i : SIZE + HALF * c + i + CH, col] = lo
        left_dot(2, 0)
        left_dot(3, 1)
        back_shift = lax.rem(HALF - s, HALF)
        fit = lane < HALF - s
        for i in range(0, HALF, CH):
            for h in range(2):
                at = HALF * h + i
                span = slice(at, at + CH)
                grads = []
                numer = []
                denom = []
                for j in range(2):
                    col = slice(HALF * j, HALF * (j + 1))
                    w = []
                    for c in range(2):
                        part = slice(HALF * c + i, HALF * c + i + CH)
                        a, b = ys[0, part, col], ys[1, part, col]
                        w.append(a - b if h else a + b)
                    pr, pi = prob[0, j, span], prob[1, j, span]
                    orr, oi = patch[0, j, span], patch[1, j, span]
                    grads.append((pr * w[0] + pi * w[1], pr * w[1] - pi * w[0]))
                    numer.append((orr * w[0] + oi * w[1], orr * w[1] - oi * w[0]))
                    denom.append(orr * orr + oi * oi)
                where = pl.ds(row + at, CH)
                for c in range(2):
                    acc_ref[c, tile, where, :] += jnp.where(ge, grads[0][c], 0.0)
                    acc_ref[c, tile + 1, where, :] += grads[1][c]
                    acc_ref[c, tile + 2, where, :] += jnp.where(ge, 0.0, grads[0][c])
                    n0, n1 = rolled(numer[0][c], numer[1][c], back_shift, fit)
                    sums_ref[c, 0, span] += n0
                    sums_ref[c, 1, span] += n1
                d0, d1 = rolled(denom[0], denom[1], back_shift, fit)
                sums_ref[2, 0, span] += d0
                sums_ref[2, 1, span] += d1
        return carry

    lax.fori_loop(0, count, body, 0)


def final_kernel(own_ref, acc_ref, illum_ref, b_ref, bi_ref, r_ref, ri_ref, out_ref):
    for t in range(4):
        for i in range(0, ROWS, CH * 2):
            rows = slice(i, i + CH * 2)
            den = illum_ref[t, rows] + 1.0
            num = [acc_ref[0, t, rows], acc_ref[1, t, rows]]
            if i < SIZE:
                den += bi_ref[t, rows]
                num = [num[c] + b_ref[c, t, rows] for c in range(2)]
            if t < 2:
                den += ri_ref[t, rows]
                num = [num[c] + r_ref[c, t, rows] for c in range(2)]
            col = slice(HALF * t, HALF * (t + 1))
            for c in range(2):
                out_ref[c, rows, col] = own_ref[c, rows, col] + num[c] / den


def shift(value, axis, step):
    count = lax.axis_size(axis)
    pairs = [(i, i + step) for i in range(count) if 0 <= i + step < count]
    return lax.ppermute(value, axis, pairs)


def smem():
    return pl.BlockSpec(memory_space=pltpu.SMEM)


def vmem():
    return pl.BlockSpec(memory_space=pltpu.VMEM)


def anywhere():
    return pl.BlockSpec(memory_space=pl.ANY)


def params():
    return pltpu.CompilerParams(vmem_limit_bytes=VMEM_LIMIT)


def rims(acc):
    lead = acc.ndim - 3
    east = lax.slice_in_dim(acc, 4, 6, axis=lead)
    corner = shift(lax.slice_in_dim(east, ROWS, ROWS + SIZE, axis=lead + 1), "tx", 1)
    right = shift(lax.slice_in_dim(east, 0, ROWS, axis=lead + 1), "tx", 1)
    south = lax.slice_in_dim(lax.slice_in_dim(acc, 0, 4, axis=lead), ROWS, ROWS + SIZE, axis=lead + 1)
    pad = jnp.concatenate(
        [
            lax.slice_in_dim(south, 0, 2, axis=lead) + corner,
            lax.slice_in_dim(south, 2, 4, axis=lead),
        ],
        lead,
    )
    return shift(pad, "ty", 1), right


def reduced(value):
    devices = lax.axis_size(AXES)
    parts = value.reshape(devices, -1, HALF)
    mine = lax.all_to_all(parts, AXES, 0, 0, tiled=True).sum(0)
    shared = lax.all_to_all(jnp.broadcast_to(mine[None], parts.shape), AXES, 0, 0, tiled=True)
    return shared.reshape(value.shape)


def local(object_field, probe, slot_counts, positions, amplitude):
    f32 = jnp.float32
    pos = positions.reshape(2, CAP)
    amps = amplitude.reshape(CAP, SIZE, SIZE)
    left, right = (jnp.asarray(t) for t in tables())

    south = shift(object_field[:, :SIZE, :], "ty", -1)
    east = shift(object_field[:, :, :SIZE], "tx", -1)
    corner = shift(south[:, :, :SIZE], "tx", -1)

    illum = pl.pallas_call(
        illum_kernel,
        out_shape=jax.ShapeDtypeStruct((6, ROWS + SIZE, HALF), f32),
        in_specs=[smem(), smem(), vmem()],
        out_specs=vmem(),
        scratch_shapes=[pltpu.VMEM((2, SIZE, HALF), f32)],
        compiler_params=params(),
        name="illum",
    )(slot_counts, pos, probe)
    illum_below, illum_right = rims(illum)

    acc, sums = pl.pallas_call(
        slots_kernel,
        out_shape=(
            jax.ShapeDtypeStruct((2, 6, ROWS + SIZE, HALF), f32),
            jax.ShapeDtypeStruct((3, 2, SIZE, HALF), f32),
        ),
        in_specs=[smem(), smem()] + [anywhere()] * 5 + [vmem()] * 3,
        out_specs=(vmem(), vmem()),
        scratch_shapes=[
            pltpu.VMEM((2, 6, ROWS + SIZE, HALF), f32),
            pltpu.VMEM((2, 2, SIZE, HALF), f32),
            pltpu.VMEM((2, 2, SIZE, HALF), f32),
            pltpu.VMEM((2, 2 * SIZE, SIZE), jnp.bfloat16),
            pltpu.VMEM((2, SIZE, SIZE), f32),
            pltpu.VMEM((2, SIZE, 2 * SIZE), jnp.bfloat16),
            pltpu.VMEM((2, SIZE, SIZE), f32),
            pltpu.VMEM((2, 2, SIZE, HALF), f32),
            pltpu.SemaphoreType.DMA((24,)),
            pltpu.SemaphoreType.DMA((2, 2)),
        ],
        compiler_params=params(),
        name="slots",
    )(slot_counts, pos, object_field, east, south, corner, amps, probe, left, right)

    below, beside = rims(acc)
    sums = reduced(sums.reshape(3 * 2 * SIZE, HALF)).reshape(3, 2, SIZE, HALF)
    new_object = pl.pallas_call(
        final_kernel,
        out_shape=jax.ShapeDtypeStruct((2, ROWS, COLS), f32),
        in_specs=[vmem()] * 7,
        out_specs=vmem(),
        compiler_params=params(),
        name="final",
    )(object_field, acc, illum, below, illum_below, beside, illum_right)
    sums = jnp.concatenate([sums[:, 0], sums[:, 1]], 2)
    new_probe = probe + sums[:2] / (sums[2][None] + 1.0)
    return (new_object, new_probe)


def solution(mesh):
    in_specs = (
        P(None, "ty", "tx"),
        P(),
        P("ty", "tx"),
        P("ty", "tx", None, None),
        P("ty", "tx", None, None, None),
    )
    out_specs = (P(None, "ty", "tx"), P())
    return jax.shard_map(local, mesh=mesh, in_specs=in_specs, out_specs=out_specs, check_vma=False)
```

```python
import functools

import jax
import jax.numpy as jnp
import ml_dtypes
import numpy as np
from jax import lax
from jax.experimental import pallas as pl
from jax.experimental.pallas import tpu as pltpu
from jax.sharding import PartitionSpec as P

SIZE = 256
HALF = 128
ROWS = 768
COLS = 512
CAP = 24
CH = 16
SPARE = ROWS + SIZE
DEEP = SPARE + SIZE
AXES = ("ty", "tx")
VMEM_LIMIT = 48 * 1024 * 1024


def halves(matrix):
    high = matrix.astype(ml_dtypes.bfloat16)
    low = (matrix - high.astype(np.float64)).astype(ml_dtypes.bfloat16)
    return high, low


def left_table(m):
    real = np.block([[m.real, -m.imag], [m.imag, m.real]])
    high, low = halves(real)
    return np.concatenate([high, high, low], 1)


def right_table(m):
    real = np.block([[m.real, m.imag], [-m.imag, m.real]])
    high, low = halves(real)
    return np.concatenate([high, high, low], 0)


@functools.lru_cache(maxsize=None)
def tables():
    n = np.arange(HALF)
    even = 2 * n
    odd_row = 2 * n + 1
    odd_col = 2 * ((n + HALF // 2) % HALF) + 1

    def dft(freq):
        turns = (freq[:, None] * n[None, :]) % SIZE
        return np.exp(-2j * np.pi * turns / SIZE) / np.sqrt(SIZE)

    left = np.stack(
        [
            left_table(dft(even)),
            left_table(dft(odd_row)),
            left_table(np.conj(dft(even)).T),
            left_table(np.conj(dft(odd_row)).T),
        ]
    )
    right = np.stack(
        [
            right_table(dft(even).T),
            right_table(dft(odd_col).T),
            right_table(np.conj(dft(even))),
            right_table(np.conj(dft(odd_col))),
        ]
    )
    return left, right


def split(x):
    high = x.astype(jnp.bfloat16)
    low = (x - high.astype(jnp.float32)).astype(jnp.bfloat16)
    return high, low


def dot(a, b):
    return jnp.dot(a, b, preferred_element_type=jnp.float32)


def lanes(rows):
    return lax.broadcasted_iota(jnp.int32, (rows, HALF), 1)


def rolled(a, b, s, low_first):
    ra = pltpu.roll(a, s, 1)
    rb = pltpu.roll(b, s, 1)
    return jnp.where(low_first, ra, rb), jnp.where(low_first, rb, ra)


def slots_kernel(inside, *refs):
    if inside:
        count_ref, pos_ref, own_ref, amp_ref, probe_ref, left_ref, right_ref = refs[:7]
        own_out, sums_out = refs[7:9]
        refs = refs[9:]
    else:
        count_ref, pos_ref, own_ref, east_ref, south_ref, corner_ref, own_in, sums_in = refs[:8]
        amp_ref, probe_ref, left_ref, right_ref = refs[8:12]
        own_out, east_out, south_out, corner_out, parts_out = refs[12:17]
        refs = refs[17:]
    todo, ext, acc, sums, work_a, work_b, amp, piece_sem, acc_sem, amp_sem = refs

    pieces = []

    def piece(source, c, t, rows):
        pieces.append(pltpu.make_async_copy(source, ext.at[c, t, rows], piece_sem.at[len(pieces)]))

    for c in range(2):
        for t in range(6):
            span = pl.ds(HALF * (t % 4), HALF)
            if t < 4:
                piece(own_ref.at[c, :, span], c, t, pl.ds(0, ROWS))
            elif not inside:
                piece(east_ref.at[c, :, span], c, t, pl.ds(0, ROWS))
            if not inside:
                piece((south_ref if t < 4 else corner_ref).at[c, :, span], c, t, pl.ds(ROWS, SIZE))
    for copy in pieces:
        copy.start()
    earlier = []
    if not inside:
        earlier = [
            pltpu.make_async_copy(own_in, acc.at[:, pl.ds(0, 4), pl.ds(0, ROWS)], acc_sem.at[0]),
            pltpu.make_async_copy(sums_in, sums.at[0], acc_sem.at[1]),
        ]
    for copy in earlier:
        copy.start()

    def choose(k, found):
        row = lax.rem(pos_ref[0, k], ROWS)
        col = lax.rem(pos_ref[1, k], COLS)
        within = jnp.where(row <= ROWS - SIZE, 1, 0) * jnp.where(col <= COLS - SIZE, 1, 0)
        todo[0, found] = k
        todo[1, found] = row
        todo[2, found] = col
        return found + (within if inside else 1 - within)

    count = lax.fori_loop(0, count_ref[0, 0], choose, 0)
    todo[0, count] = 0
    todo[1, count] = SPARE
    todo[2, count] = 0
    pairs = lax.div(count + 1, 2)

    def amp_copies(k, slot):
        return [
            pltpu.make_async_copy(amp_ref.at[k, :, pl.ds(HALF * j, HALF)], amp.at[slot, j], amp_sem.at[slot, j])
            for j in range(2)
        ]

    def fetch(n, half):
        @pl.when(n < pairs)
        def _():
            for u in range(2):
                for copy in amp_copies(todo[0, 2 * n + u], half + u):
                    copy.start()

    fetch(0, 0)
    if inside:
        acc[:, :4, :ROWS] = jnp.zeros((3, 4, ROWS, HALF), jnp.float32)
        sums[0] = jnp.zeros((3, 2, SIZE, HALF), jnp.float32)
    else:
        acc[:, 4:, :SPARE] = jnp.zeros((3, 2, SPARE, HALF), jnp.float32)
        acc[:, :4, ROWS:SPARE] = jnp.zeros((3, 4, SIZE, HALF), jnp.float32)
    for copy in pieces + earlier:
        copy.wait()
    lane = lanes(CH)
    near = lane < HALF // 2
    pick0 = jnp.where(near, 2 * lane, 2 * lane - (HALF - 1))
    pick1 = jnp.where(near, 2 * lane + 1, 2 * lane - HALF)

    def stages(n, slot, work):
        xs, ys, zs, fs, prob, patch = work
        k = todo[0, n]
        row, col = todo[1, n], todo[2, n]
        tile, s = lax.div(col, HALF), lax.rem(col, HALF)
        kept = lax.div(row, SPARE)
        ge = lane >= s
        back_shift = lax.rem(HALF - s, HALF)
        fit = lane < HALF - s

        def put_x(p, i, c, j, value):
            hi, lo = split(value)
            col = slice(HALF * j, HALF * (j + 1))
            xs[p, pl.ds(HALF * c + i, CH), col] = hi
            xs[p, pl.ds(SIZE + HALF * c + i, CH), col] = lo

        def put_z(p, rows, c, value):
            hi, lo = split(value)
            zs[p, rows, HALF * c : HALF * (c + 1)] = hi
            zs[p, rows, SIZE + HALF * c : SIZE + HALF * (c + 1)] = lo

        def left_dot(table, p):
            ys[p] = dot(left_ref[table, :, : 2 * SIZE], xs[p]) + dot(left_ref[table, :, 2 * SIZE :], xs[p, :SIZE])

        def right_dot(table, p):
            fs[p] = dot(zs[p], right_ref[table, : 2 * SIZE]) + dot(zs[p, :, :SIZE], right_ref[table, 2 * SIZE :])

        def exit_wave(i):
            waves = []
            for h in range(2):
                span = pl.ds(HALF * h + i, CH)
                pr = rolled(probe_ref[0, span, :HALF], probe_ref[0, span, HALF:], s, ge)
                pi = rolled(probe_ref[1, span, :HALF], probe_ref[1, span, HALF:], s, ge)
                where = pl.ds(row + HALF * h + i, CH)
                obj = []
                for c in range(2):
                    first = jnp.where(ge, ext[c, tile, where, :], ext[c, tile + 2, where, :])
                    obj.append((first, ext[c, tile + 1, where, :]))
                for j in range(2):
                    prob[0, j, span] = pr[j]
                    prob[1, j, span] = pi[j]
                    patch[0, j, span] = obj[0][j]
                    patch[1, j, span] = obj[1][j]
                waves.append(
                    [
                        (pr[j] * obj[0][j] - pi[j] * obj[1][j], pr[j] * obj[1][j] + pi[j] * obj[0][j])
                        for j in range(2)
                    ]
                )
            for j in range(2):
                for c in range(2):
                    top, low = waves[0][j][c], waves[1][j][c]
                    put_x(0, i, c, j, top + low)
                    put_x(1, i, c, j, top - low)

        def column_split(i):
            for r in range(2):
                rows = pl.ds(HALF * r + i, CH)
                for c in range(2):
                    span = pl.ds(HALF * c + i, CH)
                    a, b = ys[r, span, :HALF], ys[r, span, HALF:]
                    put_z(0, rows, c, a + b)
                    put_z(1, rows, c, a - b)

        def correct(i):
            for r in range(2):
                rows = pl.ds(HALF * r + i, CH)
                a0 = amp[slot, 0, pl.ds(2 * i + r, CH, stride=2), :]
                a1 = amp[slot, 1, pl.ds(2 * i + r, CH, stride=2), :]
                v0 = jnp.take_along_axis(a0, pick0, axis=1)
                v1 = jnp.take_along_axis(a1, pick1, axis=1)
                for p, value in ((0, jnp.where(near, v0, v1)), (1, jnp.where(near, v1, v0))):
                    fr, fi = fs[p, rows, :HALF], fs[p, rows, HALF:]
                    scale = value * lax.rsqrt(fr * fr + fi * fi + 0.25) - 1.0
                    put_z(p, rows, 0, fr * scale)
                    put_z(p, rows, 1, fi * scale)

        def column_join(i):
            for r in range(2):
                rows = pl.ds(HALF * r + i, CH)
                for c in range(2):
                    part = slice(HALF * c, HALF * (c + 1))
                    a, b = fs[0, rows, part], fs[1, rows, part]
                    put_x(r, i, c, 0, a + b)
                    put_x(r, i, c, 1, a - b)

        def collect(i):
            w = {}
            for j in range(2):
                col = slice(HALF * j, HALF * (j + 1))
                for c in range(2):
                    part = pl.ds(HALF * c + i, CH)
                    a, b = ys[0, part, col], ys[1, part, col]
                    w[0, j, c] = a + b
                    w[1, j, c] = a - b
            for h in range(2):
                span = pl.ds(HALF * h + i, CH)
                grads = []
                numer = []
                denom = []
                for j in range(2):
                    wr, wi = w[h, j, 0], w[h, j, 1]
                    pr, pi = prob[0, j, span], prob[1, j, span]
                    orr, oi = patch[0, j, span], patch[1, j, span]
                    grads.append((pr * wr + pi * wi, pr * wi - pi * wr, pr * pr + pi * pi))
                    numer.append((orr * wr + oi * wi, orr * wi - oi * wr, orr * orr + oi * oi))
                where = pl.ds(row + HALF * h + i, CH)
                new = []
                for c in range(3):
                    new.append(acc[c, tile, where, :] + jnp.where(ge, grads[0][c], 0.0))
                    new.append(acc[c, tile + 1, where, :] + grads[1][c])
                    new.append(acc[c, tile + 2, where, :] + jnp.where(ge, 0.0, grads[0][c]))
                for c in range(3):
                    for t in range(3):
                        acc[c, tile + t, where, :] = new[3 * c + t]
                for c in range(3):
                    n0, n1 = rolled(numer[0][c], numer[1][c], back_shift, fit)
                    sums[kept, c, 0, span] += n0
                    sums[kept, c, 1, span] += n1

        def wait():
            for copy in amp_copies(k, slot):
                copy.wait()

        starts = range(0, HALF, CH)
        pair = lambda d, t: [functools.partial(d, t, 0), functools.partial(d, t + 1, 1)]
        each = lambda f: [functools.partial(f, i) for i in starts]
        return [
            each(exit_wave),
            pair(left_dot, 0),
            each(column_split),
            pair(right_dot, 0),
            [wait] + each(correct),
            pair(right_dot, 2),
            each(column_join),
            pair(left_dot, 2),
            each(collect),
        ]

    def body(n, carry):
        half = 2 * lax.rem(n, 2)
        fetch(n + 1, 2 - half)
        first = stages(2 * n, half, work_a)
        second = stages(2 * n + 1, half + 1, work_b)
        for m in range(len(first) + 1):
            for part in (second[m - 1] if m else []) + (first[m] if m < len(first) else []):
                part()
        return carry

    lax.fori_loop(0, pairs, body, 0)
    outs = [pltpu.make_async_copy(acc.at[:, pl.ds(0, 4), pl.ds(0, ROWS)], own_out, acc_sem.at[0])]
    if inside:
        outs.append(pltpu.make_async_copy(sums.at[0], sums_out, acc_sem.at[1]))
    else:
        south, east = pl.ds(ROWS, SIZE), pl.ds(4, 2)
        outs.append(pltpu.make_async_copy(acc.at[:, east, pl.ds(0, ROWS)], east_out, acc_sem.at[1]))
        outs.append(pltpu.make_async_copy(acc.at[:, pl.ds(0, 4), south], south_out, acc_sem.at[2]))
        outs.append(pltpu.make_async_copy(acc.at[:, east, south], corner_out, acc_sem.at[3]))
    for copy in outs:
        copy.start()
    if not inside:
        for j in range(2):

            def arrange(b, carry):
                for c in range(3):
                    rows = sums[0, c, j, pl.ds(pl.multiple_of(8 * b, 8), 8)]
                    for h in range(2):
                        parts_out[64 * j + 2 * b + h, 4 * c : 4 * c + 4] = rows[4 * h : 4 * h + 4]
                return carry

            lax.fori_loop(0, SIZE // 8, arrange, 0)
    for copy in outs:
        copy.wait()


def final_kernel(own_ref, acc_ref, right_ref, below_ref, corner_ref, out_ref):
    tile = pl.program_id(0)
    block = pl.program_id(1)

    def put(num):
        den = num[2] + 1.0
        for c in range(2):
            out_ref[c] = own_ref[c] + num[c] / den

    for near in (True, False):
        for top in (True, False):

            @pl.when(((tile < 2) == near) & ((block == 0) == top))
            def _():
                num = [acc_ref[c, 0] for c in range(3)]
                if near:
                    num = [num[c] + right_ref[c, 0] for c in range(3)]
                if top:
                    num = [num[c] + below_ref[c, 0] for c in range(3)]
                if near and top:
                    num = [num[c] + corner_ref[c, 0] for c in range(3)]
                put(num)


def shift(value, down, along):
    rows, cols = (lax.axis_size(axis) for axis in AXES)
    pairs = [
        (i * cols + j, (i + down) * cols + j + along)
        for i in range(rows)
        for j in range(cols)
        if 0 <= i + down < rows and 0 <= j + along < cols
    ]
    return lax.ppermute(value, AXES, pairs)


def smem():
    return pl.BlockSpec(memory_space=pltpu.SMEM)


def vmem():
    return pl.BlockSpec(memory_space=pltpu.VMEM)


def anywhere():
    return pl.BlockSpec(memory_space=pl.ANY)


def floats(*shape):
    return jax.ShapeDtypeStruct(shape, jnp.float32)


def run_slots(inside, inputs):
    own = floats(3, 4, ROWS, HALF)
    if inside:
        out_shape = (own, floats(3, 2, SIZE, HALF))
        out_specs = (anywhere(), anywhere())
    else:
        out_shape = (
            own,
            floats(3, 2, ROWS, HALF),
            floats(3, 4, SIZE, HALF),
            floats(3, 2, SIZE, HALF),
            floats(128, 12, HALF),
        )
        out_specs = (anywhere(),) * 4 + (vmem(),)
    work = [
        pltpu.VMEM((2, 2 * SIZE, SIZE), jnp.bfloat16),
        pltpu.VMEM((2, SIZE, SIZE), jnp.float32),
        pltpu.VMEM((2, SIZE, 2 * SIZE), jnp.bfloat16),
        pltpu.VMEM((2, SIZE, SIZE), jnp.float32),
        pltpu.VMEM((2, 2, SIZE, HALF), jnp.float32),
        pltpu.VMEM((2, 2, SIZE, HALF), jnp.float32),
    ]
    slots = CAP // 3 if inside else CAP * 2 // 3
    return pl.pallas_call(
        functools.partial(slots_kernel, inside),
        out_shape=out_shape,
        in_specs=[smem()] * 2 + [anywhere()] * (len(inputs) - 5) + [vmem()] * 3,
        out_specs=out_specs,
        scratch_shapes=[
            pltpu.SMEM((3, 32), jnp.int32),
            pltpu.VMEM((2, 6, DEEP, HALF), jnp.float32),
            pltpu.VMEM((3, 6, DEEP, HALF), jnp.float32),
            pltpu.VMEM((2, 3, 2, SIZE, HALF), jnp.float32),
            work,
            work,
            pltpu.VMEM((4, 2, SIZE, HALF), jnp.float32),
            pltpu.SemaphoreType.DMA((24,)),
            pltpu.SemaphoreType.DMA((4,)),
            pltpu.SemaphoreType.DMA((4, 2)),
        ],
        compiler_params=pltpu.CompilerParams(vmem_limit_bytes=VMEM_LIMIT),
        cost_estimate=pl.CostEstimate(
            flops=slots * 48 * SIZE**3, bytes_accessed=slots * SIZE * SIZE * 4, transcendentals=slots * SIZE * SIZE
        ),
        name="slots_inside" if inside else "slots_other",
    )(*inputs)


def finish(object_field, acc, right, below, corner):
    def right_at(t, i):
        return 0, jnp.minimum(t, 1), jnp.where(t < 2, i, 2), 0

    return pl.pallas_call(
        final_kernel,
        grid=(4, 3),
        out_shape=floats(2, ROWS, COLS),
        in_specs=[
            pl.BlockSpec((2, SIZE, HALF), lambda t, i: (0, i, t)),
            pl.BlockSpec((3, 1, SIZE, HALF), lambda t, i: (0, t, i, 0)),
            pl.BlockSpec((3, 1, SIZE, HALF), right_at),
            pl.BlockSpec((3, 1, SIZE, HALF), lambda t, i: (0, t, 0, 0)),
            pl.BlockSpec((3, 1, SIZE, HALF), lambda t, i: (0, jnp.minimum(t, 1), 0, 0)),
        ],
        out_specs=pl.BlockSpec((2, SIZE, HALF), lambda t, i: (0, i, t)),
        name="final",
    )(object_field, acc, right, below, corner)


def local(object_field, probe, slot_counts, positions, amplitude):
    pos = positions.reshape(2, CAP)
    amps = amplitude.reshape(CAP, SIZE, SIZE)
    left, right = (jnp.asarray(t) for t in tables())
    south = shift(object_field[:, :SIZE, :], -1, 0)
    east = shift(object_field[:, :, :SIZE], 0, -1)
    corner = shift(object_field[:, :SIZE, :SIZE], -1, -1)
    common = (amps, probe, left, right)
    own_part, sums = run_slots(True, (slot_counts, pos, object_field) + common)
    acc, to_right, to_below, to_corner, parts = run_slots(
        False, (slot_counts, pos, object_field, east, south, corner, own_part, sums) + common
    )
    mine = lax.all_to_all(parts, AXES, 0, 0, tiled=True).sum(0).reshape(3, 4, HALF)
    new_object = finish(object_field, acc, shift(to_right, 0, 1), shift(to_below, 1, 0), shift(to_corner, 1, 1))
    me = lax.axis_index(AXES)
    held = lax.dynamic_slice(probe, (0, lax.rem(me, 64) * 4, lax.div(me, 64) * HALF), (2, 4, HALF))
    fresh = (held + mine[:2] / (mine[2][None] + 1.0)).reshape(1, 8, HALF)
    shared = lax.all_to_all(jnp.broadcast_to(fresh, (128, 8, HALF)), AXES, 0, 0, tiled=True)
    new_probe = shared.reshape(2, 64, 2, 4, HALF).transpose(2, 1, 3, 0, 4).reshape(2, SIZE, SIZE)
    return (new_object, new_probe)


def solution(mesh):
    in_specs = (
        P(None, "ty", "tx"),
        P(),
        P("ty", "tx"),
        P("ty", "tx", None, None),
        P("ty", "tx", None, None, None),
    )
    out_specs = (P(None, "ty", "tx"), P())
    return jax.shard_map(local, mesh=mesh, in_specs=in_specs, out_specs=out_specs, check_vma=False)
```

```python
import functools

import jax
import jax.numpy as jnp
import ml_dtypes
import numpy as np
from jax import lax
from jax.experimental import pallas as pl
from jax.experimental.pallas import tpu as pltpu
from jax.sharding import PartitionSpec as P

SIZE = 256
HALF = 128
ROWS = 768
COLS = 512
CAP = 24
AROUND = ((0, 1), (1, 0), (1, 1))
CH = 16
SPARE = ROWS + SIZE
DEEP = SPARE + SIZE
AXES = ("ty", "tx")
VMEM_LIMIT = 48 * 1024 * 1024


def halves(matrix):
    high = matrix.astype(ml_dtypes.bfloat16)
    low = (matrix - high.astype(np.float64)).astype(ml_dtypes.bfloat16)
    return high, low


def left_table(m):
    real = np.block([[m.real, -m.imag], [m.imag, m.real]])
    high, low = halves(real)
    return np.concatenate([high, high, low], 1)


def right_table(m):
    real = np.block([[m.real, m.imag], [-m.imag, m.real]])
    high, low = halves(real)
    return np.concatenate([high, high, low], 0)


@functools.lru_cache(maxsize=None)
def tables():
    n = np.arange(HALF)
    even = 2 * n
    odd_row = 2 * n + 1
    odd_col = 2 * ((n + HALF // 2) % HALF) + 1

    def dft(freq):
        turns = (freq[:, None] * n[None, :]) % SIZE
        return np.exp(-2j * np.pi * turns / SIZE) / np.sqrt(SIZE)

    left = np.stack(
        [
            left_table(dft(even)),
            left_table(dft(odd_row)),
            left_table(np.conj(dft(even)).T),
            left_table(np.conj(dft(odd_row)).T),
        ]
    )
    right = np.stack(
        [
            right_table(dft(even).T),
            right_table(dft(odd_col).T),
            right_table(np.conj(dft(even))),
            right_table(np.conj(dft(odd_col))),
        ]
    )
    return left, right


def split(x):
    high = x.astype(jnp.bfloat16)
    low = (x - high.astype(jnp.float32)).astype(jnp.bfloat16)
    return high, low


def dot(a, b):
    return jnp.dot(a, b, preferred_element_type=jnp.float32)


def lanes(rows):
    return lax.broadcasted_iota(jnp.int32, (rows, HALF), 1)


def rolled(a, b, s, low_first):
    ra = pltpu.roll(a, s, 1)
    rb = pltpu.roll(b, s, 1)
    return jnp.where(low_first, ra, rb), jnp.where(low_first, rb, ra)


EAST, SOUTH, INSIDE = range(3)


def slots_kernel(mode, *refs):
    count_ref, pos_ref, amp_ref, probe_ref, left_ref, right_ref, own_ref = refs[:7]
    refs = refs[7:]
    if mode == EAST:
        east_ref, own_out, east_out, sums_out = refs[:4]
        refs = refs[4:]
    elif mode == SOUTH:
        east_ref, south_ref, corner_ref, own_in, east_in, sums_in = refs[:6]
        own_out, east_out, south_out, corner_out, sums_out = refs[6:11]
        refs = refs[11:]
    else:
        own_in, sums_in, own_out, parts_out = refs[:4]
        refs = refs[4:]
    todo, ext, acc, sums, work_a, work_b, amp, piece_sem, acc_sem, amp_sem = refs

    pieces = []

    def piece(source, c, t, rows):
        pieces.append(pltpu.make_async_copy(source, ext.at[c, t, rows], piece_sem.at[len(pieces)]))

    for c in range(2):
        for t in range(6):
            span = pl.ds(HALF * (t % 4), HALF)
            if t < 4:
                piece(own_ref.at[c, :, span], c, t, pl.ds(0, ROWS))
            elif mode != INSIDE:
                piece(east_ref.at[c, :, span], c, t, pl.ds(0, ROWS))
            if mode == SOUTH:
                piece((south_ref if t < 4 else corner_ref).at[c, :, span], c, t, pl.ds(ROWS, SIZE))
    for copy in pieces:
        copy.start()
    main, south, own_tiles, east_tiles = pl.ds(0, ROWS), pl.ds(ROWS, SIZE), pl.ds(0, 4), pl.ds(4, 2)
    field = pl.ds(0, 2)
    own_acc = acc.at[:, own_tiles, main]
    east_acc = acc.at[field, east_tiles, main]
    earlier = []
    if mode != EAST:
        earlier = [
            pltpu.make_async_copy(own_in, own_acc, acc_sem.at[0]),
            pltpu.make_async_copy(sums_in, sums.at[0], acc_sem.at[1]),
        ]
    if mode == SOUTH:
        earlier.append(pltpu.make_async_copy(east_in, east_acc, acc_sem.at[2]))
    for copy in earlier:
        copy.start()

    def choose(k, found):
        row = lax.rem(pos_ref[0, k], ROWS)
        col = lax.rem(pos_ref[1, k], COLS)
        below = jnp.where(row > ROWS - SIZE, 1, 0)
        beside = jnp.where(col > COLS - SIZE, 1, 0)
        ours = (beside * (1 - below), below, (1 - below) * (1 - beside))[mode]
        todo[0, found] = k
        todo[1, found] = row
        todo[2, found] = col
        return found + ours

    count = lax.fori_loop(0, count_ref[0, 0], choose, 0)
    todo[0, count] = 0
    todo[1, count] = SPARE
    todo[2, count] = 0
    pairs = lax.div(count + 1, 2)

    def amp_copies(k, slot):
        return [
            pltpu.make_async_copy(amp_ref.at[k, :, pl.ds(HALF * j, HALF)], amp.at[slot, j], amp_sem.at[slot, j])
            for j in range(2)
        ]

    def fetch(n, half):
        @pl.when(n < pairs)
        def _():
            for u in range(2):
                for copy in amp_copies(todo[0, 2 * n + u], half + u):
                    copy.start()

    fetch(0, 0)
    if mode == EAST:
        acc[:, :, :ROWS] = jnp.zeros((3, 6, ROWS, HALF), jnp.float32)
        sums[0] = jnp.zeros((3, 2, SIZE, HALF), jnp.float32)
    elif mode == SOUTH:
        acc[:, :, ROWS:SPARE] = jnp.zeros((3, 6, SIZE, HALF), jnp.float32)
    for copy in pieces + earlier:
        copy.wait()
    lane = lanes(CH)
    near = lane < HALF // 2
    pick0 = jnp.where(near, 2 * lane, 2 * lane - (HALF - 1))
    pick1 = jnp.where(near, 2 * lane + 1, 2 * lane - HALF)

    def stages(n, slot, work):
        xs, ys, zs, fs, prob, patch = work
        k = todo[0, n]
        row, col = todo[1, n], todo[2, n]
        tile, s = lax.div(col, HALF), lax.rem(col, HALF)
        kept = lax.div(row, SPARE)
        ge = lane >= s
        back_shift = lax.rem(HALF - s, HALF)
        fit = lane < HALF - s

        def put_x(p, i, c, j, value):
            hi, lo = split(value)
            col = slice(HALF * j, HALF * (j + 1))
            xs[p, pl.ds(HALF * c + i, CH), col] = hi
            xs[p, pl.ds(SIZE + HALF * c + i, CH), col] = lo

        def put_z(p, rows, c, value):
            hi, lo = split(value)
            zs[p, rows, HALF * c : HALF * (c + 1)] = hi
            zs[p, rows, SIZE + HALF * c : SIZE + HALF * (c + 1)] = lo

        def left_dot(table, p):
            ys[p] = dot(left_ref[table, :, : 2 * SIZE], xs[p]) + dot(left_ref[table, :, 2 * SIZE :], xs[p, :SIZE])

        def right_dot(table, p):
            fs[p] = dot(zs[p], right_ref[table, : 2 * SIZE]) + dot(zs[p, :, :SIZE], right_ref[table, 2 * SIZE :])

        def exit_wave(i):
            waves = []
            for h in range(2):
                span = pl.ds(HALF * h + i, CH)
                pr = rolled(probe_ref[0, span, :HALF], probe_ref[0, span, HALF:], s, ge)
                pi = rolled(probe_ref[1, span, :HALF], probe_ref[1, span, HALF:], s, ge)
                where = pl.ds(row + HALF * h + i, CH)
                obj = []
                for c in range(2):
                    first = jnp.where(ge, ext[c, tile, where, :], ext[c, tile + 2, where, :])
                    obj.append((first, ext[c, tile + 1, where, :]))
                for j in range(2):
                    prob[0, j, span] = pr[j]
                    prob[1, j, span] = pi[j]
                    patch[0, j, span] = obj[0][j]
                    patch[1, j, span] = obj[1][j]
                waves.append(
                    [
                        (pr[j] * obj[0][j] - pi[j] * obj[1][j], pr[j] * obj[1][j] + pi[j] * obj[0][j])
                        for j in range(2)
                    ]
                )
            for j in range(2):
                for c in range(2):
                    top, low = waves[0][j][c], waves[1][j][c]
                    put_x(0, i, c, j, top + low)
                    put_x(1, i, c, j, top - low)

        def column_split(i):
            for r in range(2):
                rows = pl.ds(HALF * r + i, CH)
                for c in range(2):
                    span = pl.ds(HALF * c + i, CH)
                    a, b = ys[r, span, :HALF], ys[r, span, HALF:]
                    put_z(0, rows, c, a + b)
                    put_z(1, rows, c, a - b)

        def correct(i):
            for r in range(2):
                rows = pl.ds(HALF * r + i, CH)
                a0 = amp[slot, 0, pl.ds(2 * i + r, CH, stride=2), :]
                a1 = amp[slot, 1, pl.ds(2 * i + r, CH, stride=2), :]
                v0 = jnp.take_along_axis(a0, pick0, axis=1)
                v1 = jnp.take_along_axis(a1, pick1, axis=1)
                for p, value in ((0, jnp.where(near, v0, v1)), (1, jnp.where(near, v1, v0))):
                    fr, fi = fs[p, rows, :HALF], fs[p, rows, HALF:]
                    scale = value * lax.rsqrt(fr * fr + fi * fi + 0.25) - 1.0
                    put_z(p, rows, 0, fr * scale)
                    put_z(p, rows, 1, fi * scale)

        def column_join(i):
            for r in range(2):
                rows = pl.ds(HALF * r + i, CH)
                for c in range(2):
                    part = slice(HALF * c, HALF * (c + 1))
                    a, b = fs[0, rows, part], fs[1, rows, part]
                    put_x(r, i, c, 0, a + b)
                    put_x(r, i, c, 1, a - b)

        def collect(i):
            w = {}
            for j in range(2):
                col = slice(HALF * j, HALF * (j + 1))
                for c in range(2):
                    part = pl.ds(HALF * c + i, CH)
                    a, b = ys[0, part, col], ys[1, part, col]
                    w[0, j, c] = a + b
                    w[1, j, c] = a - b
            for h in range(2):
                span = pl.ds(HALF * h + i, CH)
                grads = []
                numer = []
                denom = []
                for j in range(2):
                    wr, wi = w[h, j, 0], w[h, j, 1]
                    pr, pi = prob[0, j, span], prob[1, j, span]
                    orr, oi = patch[0, j, span], patch[1, j, span]
                    grads.append((pr * wr + pi * wi, pr * wi - pi * wr, pr * pr + pi * pi))
                    numer.append((orr * wr + oi * wi, orr * wi - oi * wr, orr * orr + oi * oi))
                where = pl.ds(row + HALF * h + i, CH)
                new = []
                for c in range(3):
                    new.append(acc[c, tile, where, :] + jnp.where(ge, grads[0][c], 0.0))
                    new.append(acc[c, tile + 1, where, :] + grads[1][c])
                    new.append(acc[c, tile + 2, where, :] + jnp.where(ge, 0.0, grads[0][c]))
                for c in range(3):
                    for t in range(3):
                        acc[c, tile + t, where, :] = new[3 * c + t]
                for c in range(3):
                    n0, n1 = rolled(numer[0][c], numer[1][c], back_shift, fit)
                    sums[kept, c, 0, span] += n0
                    sums[kept, c, 1, span] += n1

        def wait():
            for copy in amp_copies(k, slot):
                copy.wait()

        starts = range(0, HALF, CH)
        pair = lambda d, t: [functools.partial(d, t, 0), functools.partial(d, t + 1, 1)]
        each = lambda f: [functools.partial(f, i) for i in starts]
        return [
            each(exit_wave),
            pair(left_dot, 0),
            each(column_split),
            pair(right_dot, 0),
            [wait] + each(correct),
            pair(right_dot, 2),
            each(column_join),
            pair(left_dot, 2),
            each(collect),
        ]

    def body(n, carry):
        half = 2 * lax.rem(n, 2)
        fetch(n + 1, 2 - half)
        first = stages(2 * n, half, work_a)
        second = stages(2 * n + 1, half + 1, work_b)
        for m in range(len(first) + 1):
            for part in (second[m - 1] if m else []) + (first[m] if m < len(first) else []):
                part()
        return carry

    lax.fori_loop(0, pairs, body, 0)
    outs = [pltpu.make_async_copy(own_acc, own_out, acc_sem.at[0])]
    if mode != INSIDE:
        outs.append(pltpu.make_async_copy(sums.at[0], sums_out, acc_sem.at[1]))
        outs.append(pltpu.make_async_copy(east_acc, east_out, acc_sem.at[2]))
    if mode == SOUTH:
        outs.append(pltpu.make_async_copy(acc.at[field, own_tiles, south], south_out, acc_sem.at[3]))
        outs.append(pltpu.make_async_copy(acc.at[field, east_tiles, south], corner_out, acc_sem.at[4]))
    for copy in outs:
        copy.start()
    if mode == INSIDE:
        for j in range(2):

            def arrange(b, carry):
                for c in range(3):
                    rows = sums[0, c, j, pl.ds(pl.multiple_of(8 * b, 8), 8)]
                    for h in range(2):
                        parts_out[64 * j + 2 * b + h, 4 * c : 4 * c + 4] = rows[4 * h : 4 * h + 4]
                return carry

            lax.fori_loop(0, SIZE // 8, arrange, 0)
    for copy in outs:
        copy.wait()


def light_kernel(count_ref, pos_ref, probe_ref, out_ref, todo, power, light):
    found = 0
    for n, (down, along) in enumerate(AROUND):

        def choose(k, at):
            row = lax.rem(pos_ref[n, 0, k], ROWS) - down * ROWS + SIZE
            col = lax.rem(pos_ref[n, 1, k], COLS) - along * COLS + SIZE
            todo[0, at] = row
            todo[1, at] = col
            return at + jnp.where(row > 0, 1, 0) * jnp.where(col > 0, 1, 0)

        found = lax.fori_loop(0, count_ref[n], choose, found)
    light[2:6, SIZE : SIZE + ROWS] = jnp.zeros((4, ROWS, HALF), jnp.float32)
    for j in range(2):
        re = probe_ref[0, :, HALF * j : HALF * (j + 1)]
        im = probe_ref[1, :, HALF * j : HALF * (j + 1)]
        power[j] = re * re + im * im

    def body(k, carry):
        row, col = todo[0, k], todo[1, k]
        tile, s = lax.div(col, HALF), lax.rem(col, HALF)
        ge = lanes(CH) >= s
        for i in range(0, SIZE, CH):
            p0, p1 = rolled(power[0, i : i + CH], power[1, i : i + CH], s, ge)
            at = pl.ds(row + i, CH)
            new = [
                light[tile, at, :] + jnp.where(ge, p0, 0.0),
                light[tile + 1, at, :] + p1,
                light[tile + 2, at, :] + jnp.where(ge, 0.0, p0),
            ]
            for t in range(3):
                light[tile + t, at, :] = new[t]
        return carry

    lax.fori_loop(0, found, body, 0)
    out_ref[...] = light[2:6, SIZE : SIZE + ROWS]


def calm_kernel(own_ref, acc_ref, out_ref):
    den = acc_ref[2, 0] + 1.0
    for c in range(2):
        out_ref[c] = own_ref[c] + acc_ref[c, 0] / den


def rim_kernel(calm_ref, own_ref, acc_ref, light_ref, right_ref, below_ref, corner_ref, out_ref):
    step = pl.program_id(0)

    def put(sources):
        num = [sum((ref[c, 0] for ref in sources[1:]), sources[0][c, 0]) for c in range(2)]
        den = acc_ref[2, 0] + light_ref[0] + 1.0
        for c in range(2):
            out_ref[c] = own_ref[c] + num[c] / den

    @pl.when(step < 2)
    def _():
        put((acc_ref, below_ref))

    @pl.when((step >= 2) & (step < 4))
    def _():
        put((acc_ref, right_ref, below_ref, corner_ref))

    @pl.when(step >= 4)
    def _():
        put((acc_ref, right_ref))


def shift(value, down, along):
    rows, cols = (lax.axis_size(axis) for axis in AXES)
    pairs = [
        (i * cols + j, (i + down) * cols + j + along)
        for i in range(rows)
        for j in range(cols)
        if 0 <= i + down < rows and 0 <= j + along < cols
    ]
    return lax.ppermute(value, AXES, pairs)


def smem():
    return pl.BlockSpec(memory_space=pltpu.SMEM)


def vmem():
    return pl.BlockSpec(memory_space=pltpu.VMEM)


def anywhere():
    return pl.BlockSpec(memory_space=pl.ANY)


def floats(*shape):
    return jax.ShapeDtypeStruct(shape, jnp.float32)


def run_slots(mode, common, inputs):
    own, sums = floats(3, 4, ROWS, HALF), floats(3, 2, SIZE, HALF)
    east, south, corner = floats(2, 2, ROWS, HALF), floats(2, 4, SIZE, HALF), floats(2, 2, SIZE, HALF)
    if mode == EAST:
        out_shape = (own, east, sums)
    elif mode == SOUTH:
        out_shape = (own, east, south, corner, sums)
    else:
        out_shape = (own, floats(128, 12, HALF))
    out_specs = [anywhere() for _ in out_shape]
    if mode == INSIDE:
        out_specs[1] = vmem()
    work = [
        pltpu.VMEM((2, 2 * SIZE, SIZE), jnp.bfloat16),
        pltpu.VMEM((2, SIZE, SIZE), jnp.float32),
        pltpu.VMEM((2, SIZE, 2 * SIZE), jnp.bfloat16),
        pltpu.VMEM((2, SIZE, SIZE), jnp.float32),
        pltpu.VMEM((2, 2, SIZE, HALF), jnp.float32),
        pltpu.VMEM((2, 2, SIZE, HALF), jnp.float32),
    ]
    slots = CAP // 3
    return pl.pallas_call(
        functools.partial(slots_kernel, mode),
        out_shape=out_shape,
        in_specs=[smem()] * 2 + [anywhere()] + [vmem()] * 3 + [anywhere()] * (1 + len(inputs)),
        out_specs=tuple(out_specs),
        scratch_shapes=[
            pltpu.SMEM((3, 32), jnp.int32),
            pltpu.VMEM((2, 6, DEEP, HALF), jnp.float32),
            pltpu.VMEM((3, 6, DEEP, HALF), jnp.float32),
            pltpu.VMEM((2, 3, 2, SIZE, HALF), jnp.float32),
            work,
            work,
            pltpu.VMEM((4, 2, SIZE, HALF), jnp.float32),
            pltpu.SemaphoreType.DMA((24,)),
            pltpu.SemaphoreType.DMA((5,)),
            pltpu.SemaphoreType.DMA((4, 2)),
        ],
        compiler_params=pltpu.CompilerParams(vmem_limit_bytes=VMEM_LIMIT),
        cost_estimate=pl.CostEstimate(
            flops=slots * 48 * SIZE**3, bytes_accessed=slots * SIZE * SIZE * 4, transcendentals=slots * SIZE * SIZE
        ),
        name=("slots_east", "slots_south", "slots_inside")[mode],
    )(*common, *inputs)


def update_calm(object_field, acc):
    return pl.pallas_call(
        calm_kernel,
        grid=(2, 2),
        out_shape=floats(2, ROWS, COLS),
        in_specs=[
            pl.BlockSpec((2, SIZE, HALF), lambda t, i: (0, i + 1, t + 2)),
            pl.BlockSpec((3, 1, SIZE, HALF), lambda t, i: (0, t + 2, i + 1, 0)),
        ],
        out_specs=pl.BlockSpec((2, SIZE, HALF), lambda t, i: (0, i + 1, t + 2)),
        cost_estimate=pl.CostEstimate(flops=1 << 20, bytes_accessed=4 << 20, transcendentals=0),
        name="calm",
    )(object_field, acc)


def update_rim(calm, object_field, acc, light, right, below, corner):
    def tile(n):
        return jnp.where(n < 4, 3 - n, lax.div(n - 4, 2))

    def block(n):
        return jnp.where(n < 4, 0, 1 + lax.rem(n, 2))

    return pl.pallas_call(
        rim_kernel,
        grid=(8,),
        out_shape=floats(2, ROWS, COLS),
        in_specs=[
            anywhere(),
            pl.BlockSpec((2, SIZE, HALF), lambda n: (0, block(n), tile(n))),
            pl.BlockSpec((3, 1, SIZE, HALF), lambda n: (0, tile(n), block(n), 0)),
            pl.BlockSpec((1, SIZE, HALF), lambda n: (tile(n), block(n), 0)),
            pl.BlockSpec((2, 1, SIZE, HALF), lambda n: (0, jnp.minimum(tile(n), 1), block(n), 0)),
            pl.BlockSpec((2, 1, SIZE, HALF), lambda n: (0, jnp.where(n < 4, 3 - n, 0), 0, 0)),
            pl.BlockSpec((2, 1, SIZE, HALF), lambda n: (0, jnp.where(n < 3, 1, 0), 0, 0)),
        ],
        out_specs=pl.BlockSpec((2, SIZE, HALF), lambda n: (0, block(n), tile(n))),
        input_output_aliases={0: 0},
        cost_estimate=pl.CostEstimate(flops=1 << 20, bytes_accessed=20 << 20, transcendentals=0),
        name="rim",
    )(calm, object_field, acc, light, right, below, corner)


def light_around(slot_counts, pos, probe):
    table = jnp.concatenate([pos.reshape(1, 2 * CAP), slot_counts], 1)
    table = jnp.concatenate([shift(table, down, along) for down, along in AROUND], 0)
    return pl.pallas_call(
        light_kernel,
        out_shape=floats(4, ROWS, HALF),
        in_specs=[smem(), smem(), vmem()],
        out_specs=vmem(),
        scratch_shapes=[
            pltpu.SMEM((2, 80), jnp.int32),
            pltpu.VMEM((2, SIZE, HALF), jnp.float32),
            pltpu.VMEM((8, DEEP, HALF), jnp.float32),
        ],
        compiler_params=pltpu.CompilerParams(vmem_limit_bytes=VMEM_LIMIT // 2),
        cost_estimate=pl.CostEstimate(flops=1 << 20, bytes_accessed=8 << 20, transcendentals=0),
        name="light",
    )(table[:, 2 * CAP], table[:, : 2 * CAP].reshape(3, 2, CAP), probe)


def local(object_field, probe, slot_counts, positions, amplitude):
    pos = positions.reshape(2, CAP)
    amps = amplitude.reshape(CAP, SIZE, SIZE)
    left, right = (jnp.asarray(t) for t in tables())
    east = shift(object_field[:, :, :SIZE], 0, -1)
    south = shift(object_field[:, :SIZE, :], -1, 0)
    corner = shift(object_field[:, :SIZE, :SIZE], -1, -1)
    common = (slot_counts, pos, amps, probe, left, right, object_field)
    light = light_around(slot_counts, pos, probe)
    east, light = lax.optimization_barrier((east, light))
    own_part, east_part, sums = run_slots(EAST, common, (east,))
    own_part, to_right, to_below, to_corner, sums = run_slots(
        SOUTH, common, (east, south, corner, own_part, east_part, sums)
    )
    from_left, from_above, from_corner = shift(to_right, 0, 1), shift(to_below, 1, 0), shift(to_corner, 1, 1)
    acc, parts = run_slots(INSIDE, common, (own_part, sums))
    calm = update_calm(object_field, acc)
    parts, from_left, from_above, from_corner = lax.optimization_barrier(
        (parts, from_left, from_above, from_corner)
    )
    mine = lax.all_to_all(parts, AXES, 0, 0, tiled=True).sum(0).reshape(3, 4, HALF)
    new_object = update_rim(calm, object_field, acc, light, from_left, from_above, from_corner)
    me = lax.axis_index(AXES)
    held = lax.dynamic_slice(probe, (0, lax.rem(me, 64) * 4, lax.div(me, 64) * HALF), (2, 4, HALF))
    fresh = (held + mine[:2] / (mine[2][None] + 1.0)).reshape(1, 8, HALF)
    shared = lax.all_to_all(jnp.broadcast_to(fresh, (128, 8, HALF)), AXES, 0, 0, tiled=True)
    new_probe = shared.reshape(2, 64, 2, 4, HALF).transpose(2, 1, 3, 0, 4).reshape(2, SIZE, SIZE)
    return (new_object, new_probe)


def solution(mesh):
    in_specs = (
        P(None, "ty", "tx"),
        P(),
        P("ty", "tx"),
        P("ty", "tx", None, None),
        P("ty", "tx", None, None, None),
    )
    out_specs = (P(None, "ty", "tx"), P())
    return jax.shard_map(local, mesh=mesh, in_specs=in_specs, out_specs=out_specs, check_vma=False)
```

```python
import functools

import jax
import jax.numpy as jnp
import ml_dtypes
import numpy as np
from jax import lax
from jax.experimental import pallas as pl
from jax.experimental.pallas import tpu as pltpu
from jax.sharding import PartitionSpec as P

SIZE = 256
HALF = 128
ROWS = 768
COLS = 512
CAP = 24
AROUND = ((0, 1), (1, 0), (1, 1))
CH = 16
SPARE = ROWS + SIZE
DEEP = SPARE + SIZE
AXES = ("ty", "tx")
VMEM_LIMIT = 48 * 1024 * 1024


def halves(matrix):
    high = matrix.astype(ml_dtypes.bfloat16)
    low = (matrix - high.astype(np.float64)).astype(ml_dtypes.bfloat16)
    return high, low


def left_table(m):
    real = np.block([[m.real, -m.imag], [m.imag, m.real]])
    high, low = halves(real)
    return np.concatenate([high, high, low], 1)


def right_table(m):
    real = np.block([[m.real, m.imag], [-m.imag, m.real]])
    high, low = halves(real)
    return np.concatenate([high, high, low], 0)


@functools.lru_cache(maxsize=None)
def tables():
    n = np.arange(HALF)
    even = 2 * n
    odd_row = 2 * n + 1
    odd_col = 2 * ((n + HALF // 2) % HALF) + 1

    def dft(freq):
        turns = (freq[:, None] * n[None, :]) % SIZE
        return np.exp(-2j * np.pi * turns / SIZE) / np.sqrt(SIZE)

    left = np.stack(
        [
            left_table(dft(even)),
            left_table(dft(odd_row)),
            left_table(np.conj(dft(even)).T),
            left_table(np.conj(dft(odd_row)).T),
        ]
    )
    right = np.stack(
        [
            right_table(dft(even).T),
            right_table(dft(odd_col).T),
            right_table(np.conj(dft(even))),
            right_table(np.conj(dft(odd_col))),
        ]
    )
    return left, right


def split(x):
    high = x.astype(jnp.bfloat16)
    low = (x - high.astype(jnp.float32)).astype(jnp.bfloat16)
    return high, low


def dot(a, b):
    return jnp.dot(a, b, preferred_element_type=jnp.float32)


def lanes(rows):
    return lax.broadcasted_iota(jnp.int32, (rows, HALF), 1)


def rolled(a, b, s, low_first):
    ra = pltpu.roll(a, s, 1)
    rb = pltpu.roll(b, s, 1)
    return jnp.where(low_first, ra, rb), jnp.where(low_first, rb, ra)


EAST, SOUTH, INSIDE = range(3)


def slots_kernel(mode, *refs):
    count_ref, pos_ref, amp_ref, probe_ref, left_ref, right_ref, own_ref = refs[:7]
    refs = refs[7:]
    if mode == EAST:
        east_ref, own_out, east_out, sums_out = refs[:4]
        refs = refs[4:]
    elif mode == SOUTH:
        east_ref, south_ref, corner_ref, own_in, east_in, sums_in = refs[:6]
        own_out, east_out, south_out, corner_out, sums_out = refs[6:11]
        refs = refs[11:]
    else:
        own_in, sums_in, own_out, parts_out = refs[:4]
        refs = refs[4:]
    todo, ext, acc, sums, work_a, work_b, amp, piece_sem, acc_sem, amp_sem = refs

    pieces = []

    def piece(source, c, t, rows):
        pieces.append(pltpu.make_async_copy(source, ext.at[c, t, rows], piece_sem.at[len(pieces)]))

    for c in range(2):
        for t in range(6):
            span = pl.ds(HALF * (t % 4), HALF)
            if t < 4:
                piece(own_ref.at[c, :, span], c, t, pl.ds(0, ROWS))
            elif mode != INSIDE:
                piece(east_ref.at[c, :, span], c, t, pl.ds(0, ROWS))
            if mode == SOUTH:
                piece((south_ref if t < 4 else corner_ref).at[c, :, span], c, t, pl.ds(ROWS, SIZE))
    for copy in pieces:
        copy.start()
    main, south, own_tiles, east_tiles = pl.ds(0, ROWS), pl.ds(ROWS, SIZE), pl.ds(0, 4), pl.ds(4, 2)
    field = pl.ds(0, 2)
    own_acc = acc.at[:, own_tiles, main]
    east_acc = acc.at[field, east_tiles, main]
    earlier = []
    if mode != EAST:
        earlier = [
            pltpu.make_async_copy(own_in, own_acc, acc_sem.at[0]),
            pltpu.make_async_copy(sums_in, sums.at[0], acc_sem.at[1]),
        ]
    if mode == SOUTH:
        earlier.append(pltpu.make_async_copy(east_in, east_acc, acc_sem.at[2]))
    for copy in earlier:
        copy.start()

    def choose(k, found):
        row = lax.rem(pos_ref[0, k], ROWS)
        col = lax.rem(pos_ref[1, k], COLS)
        below = jnp.where(row > ROWS - SIZE, 1, 0)
        beside = jnp.where(col > COLS - SIZE, 1, 0)
        ours = (beside * (1 - below), below, (1 - below) * (1 - beside))[mode]
        todo[0, found] = k
        todo[1, found] = row
        todo[2, found] = col
        return found + ours

    count = lax.fori_loop(0, count_ref[0, 0], choose, 0)
    todo[0, count] = 0
    todo[1, count] = SPARE
    todo[2, count] = 0
    pairs = lax.div(count + 1, 2)

    def amp_copies(k, slot):
        return [
            pltpu.make_async_copy(amp_ref.at[k, :, pl.ds(HALF * j, HALF)], amp.at[slot, j], amp_sem.at[slot, j])
            for j in range(2)
        ]

    def fetch(n, half):
        @pl.when(n < pairs)
        def _():
            for u in range(2):
                for copy in amp_copies(todo[0, 2 * n + u], half + u):
                    copy.start()

    fetch(0, 0)
    if mode == EAST:
        acc[:, :, :ROWS] = jnp.zeros((3, 6, ROWS, HALF), jnp.float32)
        sums[0] = jnp.zeros((3, 2, SIZE, HALF), jnp.float32)
    elif mode == SOUTH:
        acc[:, :, ROWS:SPARE] = jnp.zeros((3, 6, SIZE, HALF), jnp.float32)
    for copy in pieces + earlier:
        copy.wait()
    lane = lanes(CH)
    near = lane < HALF // 2
    pick0 = jnp.where(near, 2 * lane, 2 * lane - (HALF - 1))
    pick1 = jnp.where(near, 2 * lane + 1, 2 * lane - HALF)

    def stages(n, slot, work):
        xs, ys, zs, fs, prob, patch = work
        k = todo[0, n]
        row, col = todo[1, n], todo[2, n]
        tile, s = lax.div(col, HALF), lax.rem(col, HALF)
        kept = lax.div(row, SPARE)
        ge = lane >= s
        back_shift = lax.rem(HALF - s, HALF)
        fit = lane < HALF - s

        def put_x(p, i, c, j, value):
            hi, lo = split(value)
            col = slice(HALF * j, HALF * (j + 1))
            xs[p, pl.ds(HALF * c + i, CH), col] = hi
            xs[p, pl.ds(SIZE + HALF * c + i, CH), col] = lo

        def put_z(p, rows, c, value):
            hi, lo = split(value)
            zs[p, rows, HALF * c : HALF * (c + 1)] = hi
            zs[p, rows, SIZE + HALF * c : SIZE + HALF * (c + 1)] = lo

        def left_dot(table, p):
            ys[p] = dot(left_ref[table, :, : 2 * SIZE], xs[p]) + dot(left_ref[table, :, 2 * SIZE :], xs[p, :SIZE])

        def right_dot(table, p):
            fs[p] = dot(zs[p], right_ref[table, : 2 * SIZE]) + dot(zs[p, :, :SIZE], right_ref[table, 2 * SIZE :])

        def exit_wave(i):
            waves = []
            for h in range(2):
                span = pl.ds(HALF * h + i, CH)
                pr = rolled(probe_ref[0, span, :HALF], probe_ref[0, span, HALF:], s, ge)
                pi = rolled(probe_ref[1, span, :HALF], probe_ref[1, span, HALF:], s, ge)
                where = pl.ds(row + HALF * h + i, CH)
                obj = []
                for c in range(2):
                    first = jnp.where(ge, ext[c, tile, where, :], ext[c, tile + 2, where, :])
                    obj.append((first, ext[c, tile + 1, where, :]))
                for j in range(2):
                    prob[0, j, span] = pr[j]
                    prob[1, j, span] = pi[j]
                    patch[0, j, span] = obj[0][j]
                    patch[1, j, span] = obj[1][j]
                waves.append(
                    [
                        (pr[j] * obj[0][j] - pi[j] * obj[1][j], pr[j] * obj[1][j] + pi[j] * obj[0][j])
                        for j in range(2)
                    ]
                )
            for j in range(2):
                for c in range(2):
                    top, low = waves[0][j][c], waves[1][j][c]
                    put_x(0, i, c, j, top + low)
                    put_x(1, i, c, j, top - low)

        def column_split(i):
            for r in range(2):
                rows = pl.ds(HALF * r + i, CH)
                for c in range(2):
                    span = pl.ds(HALF * c + i, CH)
                    a, b = ys[r, span, :HALF], ys[r, span, HALF:]
                    put_z(0, rows, c, a + b)
                    put_z(1, rows, c, a - b)

        def correct(i):
            for r in range(2):
                rows = pl.ds(HALF * r + i, CH)
                a0 = amp[slot, 0, pl.ds(2 * i + r, CH, stride=2), :]
                a1 = amp[slot, 1, pl.ds(2 * i + r, CH, stride=2), :]
                v0 = jnp.take_along_axis(a0, pick0, axis=1)
                v1 = jnp.take_along_axis(a1, pick1, axis=1)
                for p, value in ((0, jnp.where(near, v0, v1)), (1, jnp.where(near, v1, v0))):
                    fr, fi = fs[p, rows, :HALF], fs[p, rows, HALF:]
                    scale = value * lax.rsqrt(fr * fr + fi * fi + 0.25) - 1.0
                    put_z(p, rows, 0, fr * scale)
                    put_z(p, rows, 1, fi * scale)

        def column_join(i):
            for r in range(2):
                rows = pl.ds(HALF * r + i, CH)
                for c in range(2):
                    part = slice(HALF * c, HALF * (c + 1))
                    a, b = fs[0, rows, part], fs[1, rows, part]
                    put_x(r, i, c, 0, a + b)
                    put_x(r, i, c, 1, a - b)

        def collect(i):
            w = {}
            for j in range(2):
                col = slice(HALF * j, HALF * (j + 1))
                for c in range(2):
                    part = pl.ds(HALF * c + i, CH)
                    a, b = ys[0, part, col], ys[1, part, col]
                    w[0, j, c] = a + b
                    w[1, j, c] = a - b
            for h in range(2):
                span = pl.ds(HALF * h + i, CH)
                grads = []
                numer = []
                denom = []
                for j in range(2):
                    wr, wi = w[h, j, 0], w[h, j, 1]
                    pr, pi = prob[0, j, span], prob[1, j, span]
                    orr, oi = patch[0, j, span], patch[1, j, span]
                    grads.append((pr * wr + pi * wi, pr * wi - pi * wr, pr * pr + pi * pi))
                    numer.append((orr * wr + oi * wi, orr * wi - oi * wr, orr * orr + oi * oi))
                where = pl.ds(row + HALF * h + i, CH)
                new = []
                for c in range(3):
                    new.append(acc[c, tile, where, :] + jnp.where(ge, grads[0][c], 0.0))
                    new.append(acc[c, tile + 1, where, :] + grads[1][c])
                    new.append(acc[c, tile + 2, where, :] + jnp.where(ge, 0.0, grads[0][c]))
                for c in range(3):
                    for t in range(3):
                        acc[c, tile + t, where, :] = new[3 * c + t]
                for c in range(3):
                    n0, n1 = rolled(numer[0][c], numer[1][c], back_shift, fit)
                    sums[kept, c, 0, span] += n0
                    sums[kept, c, 1, span] += n1

        def wait():
            for copy in amp_copies(k, slot):
                copy.wait()

        starts = range(0, HALF, CH)
        pair = lambda d, t: [functools.partial(d, t, 0), functools.partial(d, t + 1, 1)]
        each = lambda f: [functools.partial(f, i) for i in starts]
        return [
            each(exit_wave),
            pair(left_dot, 0),
            each(column_split),
            pair(right_dot, 0),
            [wait] + each(correct),
            pair(right_dot, 2),
            each(column_join),
            pair(left_dot, 2),
            each(collect),
        ]

    def body(n, carry):
        half = 2 * lax.rem(n, 2)
        fetch(n + 1, 2 - half)
        first = stages(2 * n, half, work_a)
        second = stages(2 * n + 1, half + 1, work_b)
        for m in range(len(first) + 1):
            for part in (second[m - 1] if m else []) + (first[m] if m < len(first) else []):
                part()
        return carry

    lax.fori_loop(0, pairs, body, 0)
    outs = [pltpu.make_async_copy(own_acc, own_out, acc_sem.at[0])]
    if mode != INSIDE:
        outs.append(pltpu.make_async_copy(sums.at[0], sums_out, acc_sem.at[1]))
        outs.append(pltpu.make_async_copy(east_acc, east_out, acc_sem.at[2]))
    if mode == SOUTH:
        outs.append(pltpu.make_async_copy(acc.at[field, own_tiles, south], south_out, acc_sem.at[3]))
        outs.append(pltpu.make_async_copy(acc.at[field, east_tiles, south], corner_out, acc_sem.at[4]))
    for copy in outs:
        copy.start()
    if mode == INSIDE:
        for j in range(2):

            def arrange(b, carry):
                for c in range(3):
                    rows = sums[0, c, j, pl.ds(pl.multiple_of(8 * b, 8), 8)]
                    for h in range(2):
                        parts_out[64 * j + 2 * b + h, 4 * c : 4 * c + 4] = rows[4 * h : 4 * h + 4]
                return carry

            lax.fori_loop(0, SIZE // 8, arrange, 0)
    for copy in outs:
        copy.wait()


def light_kernel(count_ref, pos_ref, probe_ref, out_ref, todo, power, light):
    found = 0
    for n, (down, along) in enumerate(AROUND):

        def choose(k, at):
            row = lax.rem(pos_ref[n, 0, k], ROWS) - down * ROWS + SIZE
            col = lax.rem(pos_ref[n, 1, k], COLS) - along * COLS + SIZE
            todo[0, at] = row
            todo[1, at] = col
            return at + jnp.where(row > 0, 1, 0) * jnp.where(col > 0, 1, 0)

        found = lax.fori_loop(0, count_ref[n], choose, found)
    light[2:6, SIZE : SIZE + ROWS] = jnp.zeros((4, ROWS, HALF), jnp.float32)
    for j in range(2):
        re = probe_ref[0, :, HALF * j : HALF * (j + 1)]
        im = probe_ref[1, :, HALF * j : HALF * (j + 1)]
        power[j] = re * re + im * im

    def body(k, carry):
        row, col = todo[0, k], todo[1, k]
        tile, s = lax.div(col, HALF), lax.rem(col, HALF)
        ge = lanes(CH) >= s
        for i in range(0, SIZE, CH):
            p0, p1 = rolled(power[0, i : i + CH], power[1, i : i + CH], s, ge)
            at = pl.ds(row + i, CH)
            new = [
                light[tile, at, :] + jnp.where(ge, p0, 0.0),
                light[tile + 1, at, :] + p1,
                light[tile + 2, at, :] + jnp.where(ge, 0.0, p0),
            ]
            for t in range(3):
                light[tile + t, at, :] = new[t]
        return carry

    lax.fori_loop(0, found, body, 0)
    out_ref[...] = light[2:6, SIZE : SIZE + ROWS]


def calm_kernel(own_ref, acc_ref, out_ref):
    den = acc_ref[2, 0] + 1.0
    for c in range(2):
        out_ref[c] = own_ref[c] + acc_ref[c, 0] / den


def rim_kernel(calm_ref, own_ref, acc_ref, light_ref, right_ref, below_ref, corner_ref, out_ref):
    step = pl.program_id(0)

    def put(sources):
        num = [sum((ref[c, 0] for ref in sources[1:]), sources[0][c, 0]) for c in range(2)]
        den = acc_ref[2, 0] + light_ref[0] + 1.0
        for c in range(2):
            out_ref[c] = own_ref[c] + num[c] / den

    @pl.when(step < 2)
    def _():
        put((acc_ref, below_ref))

    @pl.when((step >= 2) & (step < 4))
    def _():
        put((acc_ref, right_ref, below_ref, corner_ref))

    @pl.when(step >= 4)
    def _():
        put((acc_ref, right_ref))


def shift(value, down, along):
    rows, cols = (lax.axis_size(axis) for axis in AXES)
    pairs = [
        (i * cols + j, (i + down) * cols + j + along)
        for i in range(rows)
        for j in range(cols)
        if 0 <= i + down < rows and 0 <= j + along < cols
    ]
    return lax.ppermute(value, AXES, pairs)


def smem():
    return pl.BlockSpec(memory_space=pltpu.SMEM)


def vmem():
    return pl.BlockSpec(memory_space=pltpu.VMEM)


def anywhere():
    return pl.BlockSpec(memory_space=pl.ANY)


def floats(*shape):
    return jax.ShapeDtypeStruct(shape, jnp.float32)


def run_slots(mode, common, inputs):
    own, sums = floats(3, 4, ROWS, HALF), floats(3, 2, SIZE, HALF)
    east, south, corner = floats(2, 2, ROWS, HALF), floats(2, 4, SIZE, HALF), floats(2, 2, SIZE, HALF)
    if mode == EAST:
        out_shape = (own, east, sums)
    elif mode == SOUTH:
        out_shape = (own, east, south, corner, sums)
    else:
        out_shape = (own, floats(128, 12, HALF))
    out_specs = [anywhere() for _ in out_shape]
    if mode == INSIDE:
        out_specs[1] = vmem()
    work = [
        pltpu.VMEM((2, 2 * SIZE, SIZE), jnp.bfloat16),
        pltpu.VMEM((2, SIZE, SIZE), jnp.float32),
        pltpu.VMEM((2, SIZE, 2 * SIZE), jnp.bfloat16),
        pltpu.VMEM((2, SIZE, SIZE), jnp.float32),
        pltpu.VMEM((2, 2, SIZE, HALF), jnp.float32),
        pltpu.VMEM((2, 2, SIZE, HALF), jnp.float32),
    ]
    slots = CAP // 3
    return pl.pallas_call(
        functools.partial(slots_kernel, mode),
        out_shape=out_shape,
        in_specs=[smem()] * 2 + [anywhere()] + [vmem()] * 3 + [anywhere()] * (1 + len(inputs)),
        out_specs=tuple(out_specs),
        scratch_shapes=[
            pltpu.SMEM((3, 32), jnp.int32),
            pltpu.VMEM((2, 6, DEEP, HALF), jnp.float32),
            pltpu.VMEM((3, 6, DEEP, HALF), jnp.float32),
            pltpu.VMEM((2, 3, 2, SIZE, HALF), jnp.float32),
            work,
            work,
            pltpu.VMEM((4, 2, SIZE, HALF), jnp.float32),
            pltpu.SemaphoreType.DMA((24,)),
            pltpu.SemaphoreType.DMA((5,)),
            pltpu.SemaphoreType.DMA((4, 2)),
        ],
        compiler_params=pltpu.CompilerParams(vmem_limit_bytes=VMEM_LIMIT),
        cost_estimate=pl.CostEstimate(
            flops=slots * 48 * SIZE**3, bytes_accessed=slots * SIZE * SIZE * 4, transcendentals=slots * SIZE * SIZE
        ),
        name=("slots_east", "slots_south", "slots_inside")[mode],
    )(*common, *inputs)


def update_calm(object_field, acc):
    return pl.pallas_call(
        calm_kernel,
        grid=(2, 2),
        out_shape=floats(2, ROWS, COLS),
        in_specs=[
            pl.BlockSpec((2, SIZE, HALF), lambda t, i: (0, i + 1, t + 2)),
            pl.BlockSpec((3, 1, SIZE, HALF), lambda t, i: (0, t + 2, i + 1, 0)),
        ],
        out_specs=pl.BlockSpec((2, SIZE, HALF), lambda t, i: (0, i + 1, t + 2)),
        cost_estimate=pl.CostEstimate(flops=1 << 20, bytes_accessed=4 << 20, transcendentals=0),
        name="calm",
    )(object_field, acc)


def update_rim(calm, object_field, acc, light, right, below, corner):
    def tile(n):
        return jnp.where(n < 4, 3 - n, lax.div(n - 4, 2))

    def block(n):
        return jnp.where(n < 4, 0, 1 + lax.rem(n, 2))

    return pl.pallas_call(
        rim_kernel,
        grid=(8,),
        out_shape=floats(2, ROWS, COLS),
        in_specs=[
            anywhere(),
            pl.BlockSpec((2, SIZE, HALF), lambda n: (0, block(n), tile(n))),
            pl.BlockSpec((3, 1, SIZE, HALF), lambda n: (0, tile(n), block(n), 0)),
            pl.BlockSpec((1, SIZE, HALF), lambda n: (tile(n), block(n), 0)),
            pl.BlockSpec((2, 1, SIZE, HALF), lambda n: (0, jnp.minimum(tile(n), 1), block(n), 0)),
            pl.BlockSpec((2, 1, SIZE, HALF), lambda n: (0, jnp.where(n < 4, 3 - n, 0), 0, 0)),
            pl.BlockSpec((2, 1, SIZE, HALF), lambda n: (0, jnp.where(n < 3, 1, 0), 0, 0)),
        ],
        out_specs=pl.BlockSpec((2, SIZE, HALF), lambda n: (0, block(n), tile(n))),
        input_output_aliases={0: 0},
        cost_estimate=pl.CostEstimate(flops=1 << 20, bytes_accessed=20 << 20, transcendentals=0),
        name="rim",
    )(calm, object_field, acc, light, right, below, corner)


def light_around(slot_counts, pos, probe):
    table = jnp.concatenate([pos.reshape(1, 2 * CAP), slot_counts], 1)
    table = jnp.concatenate([shift(table, down, along) for down, along in AROUND], 0)
    return pl.pallas_call(
        light_kernel,
        out_shape=floats(4, ROWS, HALF),
        in_specs=[smem(), smem(), vmem()],
        out_specs=vmem(),
        scratch_shapes=[
            pltpu.SMEM((2, 80), jnp.int32),
            pltpu.VMEM((2, SIZE, HALF), jnp.float32),
            pltpu.VMEM((8, DEEP, HALF), jnp.float32),
        ],
        compiler_params=pltpu.CompilerParams(vmem_limit_bytes=VMEM_LIMIT // 2),
        cost_estimate=pl.CostEstimate(flops=1 << 20, bytes_accessed=8 << 20, transcendentals=0),
        name="light",
    )(table[:, 2 * CAP], table[:, : 2 * CAP].reshape(3, 2, CAP), probe)


def local(object_field, probe, slot_counts, positions, amplitude):
    pos = positions.reshape(2, CAP)
    amps = amplitude.reshape(CAP, SIZE, SIZE)
    left, right = (jnp.asarray(t) for t in tables())
    east = shift(object_field[:, :, :SIZE], 0, -1)
    south = shift(object_field[:, :SIZE, :], -1, 0)
    corner = shift(object_field[:, :SIZE, :SIZE], -1, -1)
    common = (slot_counts, pos, amps, probe, left, right, object_field)
    light = light_around(slot_counts, pos, probe)
    east, light = lax.optimization_barrier((east, light))
    own_part, east_part, sums = run_slots(EAST, common, (east,))
    own_part, to_right, to_below, to_corner, sums = run_slots(
        SOUTH, common, (east, south, corner, own_part, east_part, sums)
    )
    from_left, from_above, from_corner = shift(to_right, 0, 1), shift(to_below, 1, 0), shift(to_corner, 1, 1)
    acc, parts = run_slots(INSIDE, common, (own_part, sums))
    calm = update_calm(object_field, acc)
    parts, calm, from_left, from_above, from_corner = lax.optimization_barrier(
        (parts, calm, from_left, from_above, from_corner)
    )
    mine = lax.all_to_all(parts, AXES, 0, 0, tiled=True).sum(0).reshape(3, 4, HALF)
    new_object = update_rim(calm, object_field, acc, light, from_left, from_above, from_corner)
    me = lax.axis_index(AXES)
    held = lax.dynamic_slice(probe, (0, lax.rem(me, 64) * 4, lax.div(me, 64) * HALF), (2, 4, HALF))
    fresh = (held + mine[:2] / (mine[2][None] + 1.0)).reshape(1, 8, HALF)
    shared = lax.all_to_all(jnp.broadcast_to(fresh, (128, 8, HALF)), AXES, 0, 0, tiled=True)
    new_probe = shared.reshape(2, 64, 2, 4, HALF).transpose(2, 1, 3, 0, 4).reshape(2, SIZE, SIZE)
    return (new_object, new_probe)


def solution(mesh):
    in_specs = (
        P(None, "ty", "tx"),
        P(),
        P("ty", "tx"),
        P("ty", "tx", None, None),
        P("ty", "tx", None, None, None),
    )
    out_specs = (P(None, "ty", "tx"), P())
    return jax.shard_map(local, mesh=mesh, in_specs=in_specs, out_specs=out_specs, check_vma=False)
```

```python
import functools

import jax
import jax.numpy as jnp
import ml_dtypes
import numpy as np
from jax import lax
from jax.experimental import pallas as pl
from jax.experimental.pallas import tpu as pltpu
from jax.sharding import PartitionSpec as P

SIZE = 256
HALF = 128
ROWS = 768
COLS = 512
CAP = 24
AROUND = ((0, 1), (1, 0), (1, 1))
CH = 16
SPARE = ROWS + SIZE
DEEP = SPARE + SIZE
AXES = ("ty", "tx")
VMEM_LIMIT = 48 * 1024 * 1024


def halves(matrix):
    high = matrix.astype(ml_dtypes.bfloat16)
    low = (matrix - high.astype(np.float64)).astype(ml_dtypes.bfloat16)
    return high, low


def left_table(m):
    real = np.block([[m.real, -m.imag], [m.imag, m.real]])
    high, low = halves(real)
    return np.concatenate([high, high, low], 1)


def right_table(m):
    real = np.block([[m.real, m.imag], [-m.imag, m.real]])
    high, low = halves(real)
    return np.concatenate([high, high, low], 0)


@functools.lru_cache(maxsize=None)
def tables():
    n = np.arange(HALF)
    even = 2 * n
    odd_row = 2 * n + 1
    odd_col = 2 * ((n + HALF // 2) % HALF) + 1

    def dft(freq):
        turns = (freq[:, None] * n[None, :]) % SIZE
        return np.exp(-2j * np.pi * turns / SIZE) / np.sqrt(SIZE)

    left = np.stack(
        [
            left_table(dft(even)),
            left_table(dft(odd_row)),
            left_table(np.conj(dft(even)).T),
            left_table(np.conj(dft(odd_row)).T),
        ]
    )
    right = np.stack(
        [
            right_table(dft(even).T),
            right_table(dft(odd_col).T),
            right_table(np.conj(dft(even))),
            right_table(np.conj(dft(odd_col))),
        ]
    )
    return left, right


def split(x):
    high = x.astype(jnp.bfloat16)
    low = (x - high.astype(jnp.float32)).astype(jnp.bfloat16)
    return high, low


def dot(a, b):
    return jnp.dot(a, b, preferred_element_type=jnp.float32)


def lanes(rows):
    return lax.broadcasted_iota(jnp.int32, (rows, HALF), 1)


def rolled(a, b, s, low_first):
    ra = pltpu.roll(a, s, 1)
    rb = pltpu.roll(b, s, 1)
    return jnp.where(low_first, ra, rb), jnp.where(low_first, rb, ra)


EAST, SOUTH, INSIDE = range(3)


def slots_kernel(mode, *refs):
    count_ref, pos_ref, amp_ref, probe_ref, left_ref, right_ref, own_ref = refs[:7]
    refs = refs[7:]
    if mode == EAST:
        east_ref, own_out, east_out, sums_out = refs[:4]
        refs = refs[4:]
    elif mode == SOUTH:
        east_ref, south_ref, corner_ref, own_in, east_in, sums_in = refs[:6]
        own_out, east_out, south_out, corner_out, sums_out = refs[6:11]
        refs = refs[11:]
    else:
        own_in, sums_in, own_out, parts_out = refs[:4]
        refs = refs[4:]
    todo, ext, acc, sums, work_a, work_b, amp, piece_sem, acc_sem, amp_sem = refs

    pieces = []

    def piece(source, c, t, rows):
        pieces.append(pltpu.make_async_copy(source, ext.at[c, t, rows], piece_sem.at[len(pieces)]))

    for c in range(2):
        for t in range(6):
            span = pl.ds(HALF * (t % 4), HALF)
            if t < 4:
                piece(own_ref.at[c, :, span], c, t, pl.ds(0, ROWS))
            elif mode != INSIDE:
                piece(east_ref.at[c, :, span], c, t, pl.ds(0, ROWS))
            if mode == SOUTH:
                piece((south_ref if t < 4 else corner_ref).at[c, :, span], c, t, pl.ds(ROWS, SIZE))
    for copy in pieces:
        copy.start()
    main, south, own_tiles, east_tiles = pl.ds(0, ROWS), pl.ds(ROWS, SIZE), pl.ds(0, 4), pl.ds(4, 2)
    field = pl.ds(0, 2)
    own_acc = acc.at[:, own_tiles, main]
    east_acc = acc.at[field, east_tiles, main]
    earlier = []
    if mode != EAST:
        earlier = [
            pltpu.make_async_copy(own_in, own_acc, acc_sem.at[0]),
            pltpu.make_async_copy(sums_in, sums.at[0], acc_sem.at[1]),
        ]
    if mode == SOUTH:
        earlier.append(pltpu.make_async_copy(east_in, east_acc, acc_sem.at[2]))
    for copy in earlier:
        copy.start()

    def choose(k, found):
        row = lax.rem(pos_ref[0, k], ROWS)
        col = lax.rem(pos_ref[1, k], COLS)
        below = jnp.where(row > ROWS - SIZE, 1, 0)
        beside = jnp.where(col > COLS - SIZE, 1, 0)
        ours = (beside * (1 - below), below, (1 - below) * (1 - beside))[mode]
        todo[0, found] = k
        todo[1, found] = row
        todo[2, found] = col
        return found + ours

    count = lax.fori_loop(0, count_ref[0, 0], choose, 0)
    todo[0, count] = 0
    todo[1, count] = SPARE
    todo[2, count] = 0
    pairs = lax.div(count + 1, 2)

    def amp_copies(k, slot):
        return [
            pltpu.make_async_copy(amp_ref.at[k, :, pl.ds(HALF * j, HALF)], amp.at[slot, j], amp_sem.at[slot, j])
            for j in range(2)
        ]

    def fetch(n, half):
        @pl.when(n < pairs)
        def _():
            for u in range(2):
                for copy in amp_copies(todo[0, 2 * n + u], half + u):
                    copy.start()

    fetch(0, 0)
    if mode == EAST:
        acc[:, :, :ROWS] = jnp.zeros((3, 6, ROWS, HALF), jnp.float32)
        sums[0] = jnp.zeros((3, 2, SIZE, HALF), jnp.float32)
    elif mode == SOUTH:
        acc[:, :, ROWS:SPARE] = jnp.zeros((3, 6, SIZE, HALF), jnp.float32)
    for copy in pieces + earlier:
        copy.wait()
    lane = lanes(CH)
    near = lane < HALF // 2
    pick0 = jnp.where(near, 2 * lane, 2 * lane - (HALF - 1))
    pick1 = jnp.where(near, 2 * lane + 1, 2 * lane - HALF)

    def stages(n, slot, work):
        xs, ys, zs, fs, prob, patch = work
        k = todo[0, n]
        row, col = todo[1, n], todo[2, n]
        tile, s = lax.div(col, HALF), lax.rem(col, HALF)
        kept = lax.div(row, SPARE)
        ge = lane >= s
        back_shift = lax.rem(HALF - s, HALF)
        fit = lane < HALF - s

        def put_x(p, i, c, j, value):
            hi, lo = split(value)
            col = slice(HALF * j, HALF * (j + 1))
            xs[p, pl.ds(HALF * c + i, CH), col] = hi
            xs[p, pl.ds(SIZE + HALF * c + i, CH), col] = lo

        def put_z(p, rows, c, value):
            hi, lo = split(value)
            zs[p, rows, HALF * c : HALF * (c + 1)] = hi
            zs[p, rows, SIZE + HALF * c : SIZE + HALF * (c + 1)] = lo

        def left_dot(table, p):
            ys[p] = dot(left_ref[table, :, : 2 * SIZE], xs[p]) + dot(left_ref[table, :, 2 * SIZE :], xs[p, :SIZE])

        def right_dot(table, p):
            fs[p] = dot(zs[p], right_ref[table, : 2 * SIZE]) + dot(zs[p, :, :SIZE], right_ref[table, 2 * SIZE :])

        def exit_wave(i):
            waves = []
            for h in range(2):
                span = pl.ds(HALF * h + i, CH)
                pr = rolled(probe_ref[0, span, :HALF], probe_ref[0, span, HALF:], s, ge)
                pi = rolled(probe_ref[1, span, :HALF], probe_ref[1, span, HALF:], s, ge)
                where = pl.ds(row + HALF * h + i, CH)
                obj = []
                for c in range(2):
                    first = jnp.where(ge, ext[c, tile, where, :], ext[c, tile + 2, where, :])
                    obj.append((first, ext[c, tile + 1, where, :]))
                for j in range(2):
                    prob[0, j, span] = pr[j]
                    prob[1, j, span] = pi[j]
                    patch[0, j, span] = obj[0][j]
                    patch[1, j, span] = obj[1][j]
                waves.append(
                    [
                        (pr[j] * obj[0][j] - pi[j] * obj[1][j], pr[j] * obj[1][j] + pi[j] * obj[0][j])
                        for j in range(2)
                    ]
                )
            for j in range(2):
                for c in range(2):
                    top, low = waves[0][j][c], waves[1][j][c]
                    put_x(0, i, c, j, top + low)
                    put_x(1, i, c, j, top - low)

        def column_split(i):
            for r in range(2):
                rows = pl.ds(HALF * r + i, CH)
                for c in range(2):
                    span = pl.ds(HALF * c + i, CH)
                    a, b = ys[r, span, :HALF], ys[r, span, HALF:]
                    put_z(0, rows, c, a + b)
                    put_z(1, rows, c, a - b)

        def correct(i):
            for r in range(2):
                rows = pl.ds(HALF * r + i, CH)
                a0 = amp[slot, 0, pl.ds(2 * i + r, CH, stride=2), :]
                a1 = amp[slot, 1, pl.ds(2 * i + r, CH, stride=2), :]
                v0 = jnp.take_along_axis(a0, pick0, axis=1)
                v1 = jnp.take_along_axis(a1, pick1, axis=1)
                for p, value in ((0, jnp.where(near, v0, v1)), (1, jnp.where(near, v1, v0))):
                    fr, fi = fs[p, rows, :HALF], fs[p, rows, HALF:]
                    scale = value * lax.rsqrt(fr * fr + fi * fi + 0.25) - 1.0
                    put_z(p, rows, 0, fr * scale)
                    put_z(p, rows, 1, fi * scale)

        def column_join(i):
            for r in range(2):
                rows = pl.ds(HALF * r + i, CH)
                for c in range(2):
                    part = slice(HALF * c, HALF * (c + 1))
                    a, b = fs[0, rows, part], fs[1, rows, part]
                    put_x(r, i, c, 0, a + b)
                    put_x(r, i, c, 1, a - b)

        def collect(i):
            w = {}
            for j in range(2):
                col = slice(HALF * j, HALF * (j + 1))
                for c in range(2):
                    part = pl.ds(HALF * c + i, CH)
                    a, b = ys[0, part, col], ys[1, part, col]
                    w[0, j, c] = a + b
                    w[1, j, c] = a - b
            for h in range(2):
                span = pl.ds(HALF * h + i, CH)
                grads = []
                numer = []
                denom = []
                for j in range(2):
                    wr, wi = w[h, j, 0], w[h, j, 1]
                    pr, pi = prob[0, j, span], prob[1, j, span]
                    orr, oi = patch[0, j, span], patch[1, j, span]
                    grads.append((pr * wr + pi * wi, pr * wi - pi * wr, pr * pr + pi * pi))
                    numer.append((orr * wr + oi * wi, orr * wi - oi * wr, orr * orr + oi * oi))
                where = pl.ds(row + HALF * h + i, CH)
                new = []
                for c in range(3):
                    new.append(acc[c, tile, where, :] + jnp.where(ge, grads[0][c], 0.0))
                    new.append(acc[c, tile + 1, where, :] + grads[1][c])
                    new.append(acc[c, tile + 2, where, :] + jnp.where(ge, 0.0, grads[0][c]))
                for c in range(3):
                    for t in range(3):
                        acc[c, tile + t, where, :] = new[3 * c + t]
                for c in range(3):
                    n0, n1 = rolled(numer[0][c], numer[1][c], back_shift, fit)
                    sums[kept, c, 0, span] += n0
                    sums[kept, c, 1, span] += n1

        def wait():
            for copy in amp_copies(k, slot):
                copy.wait()

        starts = range(0, HALF, CH)
        pair = lambda d, t: [functools.partial(d, t, 0), functools.partial(d, t + 1, 1)]
        each = lambda f: [functools.partial(f, i) for i in starts]
        return [
            each(exit_wave),
            pair(left_dot, 0),
            each(column_split),
            pair(right_dot, 0),
            [wait] + each(correct),
            pair(right_dot, 2),
            each(column_join),
            pair(left_dot, 2),
            each(collect),
        ]

    def body(n, carry):
        half = 2 * lax.rem(n, 2)
        fetch(n + 1, 2 - half)
        first = stages(2 * n, half, work_a)
        second = stages(2 * n + 1, half + 1, work_b)
        for m in range(len(first) + 1):
            for part in (second[m - 1] if m else []) + (first[m] if m < len(first) else []):
                part()
        return carry

    lax.fori_loop(0, pairs, body, 0)
    outs = [pltpu.make_async_copy(own_acc, own_out, acc_sem.at[0])]
    if mode != INSIDE:
        outs.append(pltpu.make_async_copy(sums.at[0], sums_out, acc_sem.at[1]))
        outs.append(pltpu.make_async_copy(east_acc, east_out, acc_sem.at[2]))
    if mode == SOUTH:
        outs.append(pltpu.make_async_copy(acc.at[field, own_tiles, south], south_out, acc_sem.at[3]))
        outs.append(pltpu.make_async_copy(acc.at[field, east_tiles, south], corner_out, acc_sem.at[4]))
    for copy in outs:
        copy.start()
    if mode == INSIDE:
        for j in range(2):

            def arrange(b, carry):
                for c in range(3):
                    rows = sums[0, c, j, pl.ds(pl.multiple_of(8 * b, 8), 8)]
                    for h in range(2):
                        parts_out[64 * j + 2 * b + h, 4 * c : 4 * c + 4] = rows[4 * h : 4 * h + 4]
                return carry

            lax.fori_loop(0, SIZE // 8, arrange, 0)
    for copy in outs:
        copy.wait()


def light_kernel(count_ref, pos_ref, probe_ref, out_ref, todo, power, light):
    found = 0
    for n, (down, along) in enumerate(AROUND):

        def choose(k, at):
            row = lax.rem(pos_ref[n, 0, k], ROWS) - down * ROWS + SIZE
            col = lax.rem(pos_ref[n, 1, k], COLS) - along * COLS + SIZE
            todo[0, at] = row
            todo[1, at] = col
            return at + jnp.where(row > 0, 1, 0) * jnp.where(col > 0, 1, 0)

        found = lax.fori_loop(0, count_ref[n], choose, found)
    light[2:6, SIZE : SIZE + ROWS] = jnp.zeros((4, ROWS, HALF), jnp.float32)
    for j in range(2):
        re = probe_ref[0, :, HALF * j : HALF * (j + 1)]
        im = probe_ref[1, :, HALF * j : HALF * (j + 1)]
        power[j] = re * re + im * im

    def body(k, carry):
        row, col = todo[0, k], todo[1, k]
        tile, s = lax.div(col, HALF), lax.rem(col, HALF)
        ge = lanes(CH) >= s
        for i in range(0, SIZE, CH):
            p0, p1 = rolled(power[0, i : i + CH], power[1, i : i + CH], s, ge)
            at = pl.ds(row + i, CH)
            new = [
                light[tile, at, :] + jnp.where(ge, p0, 0.0),
                light[tile + 1, at, :] + p1,
                light[tile + 2, at, :] + jnp.where(ge, 0.0, p0),
            ]
            for t in range(3):
                light[tile + t, at, :] = new[t]
        return carry

    lax.fori_loop(0, found, body, 0)
    out_ref[...] = light[2:6, SIZE : SIZE + ROWS]


def calm_kernel(own_ref, acc_ref, out_ref):
    den = acc_ref[2, 0] + 1.0
    for c in range(2):
        out_ref[c] = own_ref[c] + acc_ref[c, 0] / den


def rim_kernel(calm_ref, own_ref, acc_ref, light_ref, right_ref, below_ref, corner_ref, out_ref):
    step = pl.program_id(0)

    def put(sources):
        num = [sum((ref[c, 0] for ref in sources[1:]), sources[0][c, 0]) for c in range(2)]
        den = acc_ref[2, 0] + light_ref[0] + 1.0
        for c in range(2):
            out_ref[c] = own_ref[c] + num[c] / den

    @pl.when(step < 2)
    def _():
        put((acc_ref, below_ref))

    @pl.when((step >= 2) & (step < 4))
    def _():
        put((acc_ref, right_ref, below_ref, corner_ref))

    @pl.when(step >= 4)
    def _():
        put((acc_ref, right_ref))


def shift(value, down, along):
    rows, cols = (lax.axis_size(axis) for axis in AXES)
    pairs = [
        (i * cols + j, (i + down) * cols + j + along)
        for i in range(rows)
        for j in range(cols)
        if 0 <= i + down < rows and 0 <= j + along < cols
    ]
    return lax.ppermute(value, AXES, pairs)


def smem():
    return pl.BlockSpec(memory_space=pltpu.SMEM)


def vmem():
    return pl.BlockSpec(memory_space=pltpu.VMEM)


def anywhere():
    return pl.BlockSpec(memory_space=pl.ANY)


def floats(*shape):
    return jax.ShapeDtypeStruct(shape, jnp.float32)


def run_slots(mode, common, inputs):
    own, sums = floats(3, 4, ROWS, HALF), floats(3, 2, SIZE, HALF)
    east, south, corner = floats(2, 2, ROWS, HALF), floats(2, 4, SIZE, HALF), floats(2, 2, SIZE, HALF)
    if mode == EAST:
        out_shape = (own, east, sums)
    elif mode == SOUTH:
        out_shape = (own, east, south, corner, sums)
    else:
        out_shape = (own, floats(128, 12, HALF))
    out_specs = [anywhere() for _ in out_shape]
    if mode == INSIDE:
        out_specs[1] = vmem()
    work = [
        pltpu.VMEM((2, 2 * SIZE, SIZE), jnp.bfloat16),
        pltpu.VMEM((2, SIZE, SIZE), jnp.float32),
        pltpu.VMEM((2, SIZE, 2 * SIZE), jnp.bfloat16),
        pltpu.VMEM((2, SIZE, SIZE), jnp.float32),
        pltpu.VMEM((2, 2, SIZE, HALF), jnp.float32),
        pltpu.VMEM((2, 2, SIZE, HALF), jnp.float32),
    ]
    slots = CAP // 3
    return pl.pallas_call(
        functools.partial(slots_kernel, mode),
        out_shape=out_shape,
        in_specs=[smem()] * 2 + [anywhere()] + [vmem()] * 3 + [anywhere()] * (1 + len(inputs)),
        out_specs=tuple(out_specs),
        scratch_shapes=[
            pltpu.SMEM((3, 32), jnp.int32),
            pltpu.VMEM((2, 6, DEEP, HALF), jnp.float32),
            pltpu.VMEM((3, 6, DEEP, HALF), jnp.float32),
            pltpu.VMEM((2, 3, 2, SIZE, HALF), jnp.float32),
            work,
            work,
            pltpu.VMEM((4, 2, SIZE, HALF), jnp.float32),
            pltpu.SemaphoreType.DMA((24,)),
            pltpu.SemaphoreType.DMA((5,)),
            pltpu.SemaphoreType.DMA((4, 2)),
        ],
        compiler_params=pltpu.CompilerParams(vmem_limit_bytes=VMEM_LIMIT),
        cost_estimate=pl.CostEstimate(
            flops=slots * 48 * SIZE**3, bytes_accessed=slots * SIZE * SIZE * 4, transcendentals=slots * SIZE * SIZE
        ),
        name=("slots_east", "slots_south", "slots_inside")[mode],
    )(*common, *inputs)


def update_calm(object_field, acc):
    return pl.pallas_call(
        calm_kernel,
        grid=(2, 2),
        out_shape=floats(2, ROWS, COLS),
        in_specs=[
            pl.BlockSpec((2, SIZE, HALF), lambda t, i: (0, i + 1, t + 2)),
            pl.BlockSpec((3, 1, SIZE, HALF), lambda t, i: (0, t + 2, i + 1, 0)),
        ],
        out_specs=pl.BlockSpec((2, SIZE, HALF), lambda t, i: (0, i + 1, t + 2)),
        cost_estimate=pl.CostEstimate(flops=1 << 20, bytes_accessed=4 << 20, transcendentals=0),
        name="calm",
    )(object_field, acc)


def update_rim(calm, object_field, acc, light, right, below, corner):
    def tile(n):
        return jnp.where(n < 4, 3 - n, lax.div(n - 4, 2))

    def block(n):
        return jnp.where(n < 4, 0, 1 + lax.rem(n, 2))

    return pl.pallas_call(
        rim_kernel,
        grid=(8,),
        out_shape=floats(2, ROWS, COLS),
        in_specs=[
            anywhere(),
            pl.BlockSpec((2, SIZE, HALF), lambda n: (0, block(n), tile(n))),
            pl.BlockSpec((3, 1, SIZE, HALF), lambda n: (0, tile(n), block(n), 0)),
            pl.BlockSpec((1, SIZE, HALF), lambda n: (tile(n), block(n), 0)),
            pl.BlockSpec((2, 1, SIZE, HALF), lambda n: (0, jnp.minimum(tile(n), 1), block(n), 0)),
            pl.BlockSpec((2, 1, SIZE, HALF), lambda n: (0, jnp.where(n < 4, 3 - n, 0), 0, 0)),
            pl.BlockSpec((2, 1, SIZE, HALF), lambda n: (0, jnp.where(n < 3, 1, 0), 0, 0)),
        ],
        out_specs=pl.BlockSpec((2, SIZE, HALF), lambda n: (0, block(n), tile(n))),
        input_output_aliases={0: 0},
        cost_estimate=pl.CostEstimate(flops=1 << 20, bytes_accessed=20 << 20, transcendentals=0),
        name="rim",
    )(calm, object_field, acc, light, right, below, corner)


def light_around(slot_counts, pos, probe):
    table = jnp.concatenate([pos.reshape(1, 2 * CAP), slot_counts], 1)
    table = jnp.concatenate([shift(table, down, along) for down, along in AROUND], 0)
    return pl.pallas_call(
        light_kernel,
        out_shape=floats(4, ROWS, HALF),
        in_specs=[smem(), smem(), vmem()],
        out_specs=vmem(),
        scratch_shapes=[
            pltpu.SMEM((2, 80), jnp.int32),
            pltpu.VMEM((2, SIZE, HALF), jnp.float32),
            pltpu.VMEM((8, DEEP, HALF), jnp.float32),
        ],
        compiler_params=pltpu.CompilerParams(vmem_limit_bytes=VMEM_LIMIT // 2),
        cost_estimate=pl.CostEstimate(flops=1 << 20, bytes_accessed=8 << 20, transcendentals=0),
        name="light",
    )(table[:, 2 * CAP], table[:, : 2 * CAP].reshape(3, 2, CAP), probe)


def local(object_field, probe, slot_counts, positions, amplitude):
    pos = positions.reshape(2, CAP)
    amps = amplitude.reshape(CAP, SIZE, SIZE)
    left, right = (jnp.asarray(t) for t in tables())
    east = shift(object_field[:, :, :SIZE], 0, -1)
    south = shift(object_field[:, :SIZE, :], -1, 0)
    corner = shift(object_field[:, :SIZE, :SIZE], -1, -1)
    common = (slot_counts, pos, amps, probe, left, right, object_field)
    light = light_around(slot_counts, pos, probe)
    east, light = lax.optimization_barrier((east, light))
    own_part, east_part, sums = run_slots(EAST, common, (east,))
    own_part, to_right, to_below, to_corner, sums = run_slots(
        SOUTH, common, (east, south, corner, own_part, east_part, sums)
    )
    from_above, from_corner, from_left = shift(to_below, 1, 0), shift(to_corner, 1, 1), shift(to_right, 0, 1)
    acc, parts = run_slots(INSIDE, common, (own_part, sums))
    calm = update_calm(object_field, acc)
    parts, calm, from_left, from_above, from_corner = lax.optimization_barrier(
        (parts, calm, from_left, from_above, from_corner)
    )
    mine = lax.all_to_all(parts, AXES, 0, 0, tiled=True).sum(0).reshape(3, 4, HALF)
    new_object = update_rim(calm, object_field, acc, light, from_left, from_above, from_corner)
    me = lax.axis_index(AXES)
    held = lax.dynamic_slice(probe, (0, lax.rem(me, 64) * 4, lax.div(me, 64) * HALF), (2, 4, HALF))
    fresh = (held + mine[:2] / (mine[2][None] + 1.0)).reshape(1, 8, HALF)
    shared = lax.all_to_all(jnp.broadcast_to(fresh, (128, 8, HALF)), AXES, 0, 0, tiled=True)
    new_probe = shared.reshape(2, 64, 2, 4, HALF).transpose(2, 1, 3, 0, 4).reshape(2, SIZE, SIZE)
    return (new_object, new_probe)


def solution(mesh):
    in_specs = (
        P(None, "ty", "tx"),
        P(),
        P("ty", "tx"),
        P("ty", "tx", None, None),
        P("ty", "tx", None, None, None),
    )
    out_specs = (P(None, "ty", "tx"), P())
    return jax.shard_map(local, mesh=mesh, in_specs=in_specs, out_specs=out_specs, check_vma=False)
```
